256 devices in a mesh: dp: 16 (over y, z_lo), factor: 16 (over z_hi, x, core).
Axes of the slice: x: 4, y: 4, z: 8 (z_hi: 2, z_lo: 4; z = z_hi * 4 + z_lo), core: 2. Of those that a mesh axis runs over, the one named last changes fastest.
Arguments:
- inputs: bfloat16 [16384, 8192], P('dp', 'factor'), may hold values from -6 to 6
- cotangent: bfloat16 [16384, 8192], P('dp', 'factor'), may hold values from -6 to 6
- first_factor: bfloat16 [64, 128, 128], P('factor'), may hold values from -0.5 to 0.5
- second_factor: bfloat16 [64, 128, 512], P('factor'), may hold values from -0.5 to 0.5
- third_factor: bfloat16 [64, 512, 128], P('factor'), may hold values from -0.25 to 0.25
- fourth_factor: bfloat16 [64, 128, 128], P('factor'), may hold values from -0.5 to 0.5
Outputs:
- result: bfloat16 [16384, 8192], P('dp', 'factor')
- input_grad: bfloat16 [16384, 8192], P('dp', 'factor')
- first_grad: float32 [64, 128, 128], P('factor', 'dp')
- second_grad: float32 [64, 128, 512], P('factor', 'dp')
- third_grad: float32 [64, 512, 128], P('factor', 'dp')
- fourth_grad: float32 [64, 128, 128], P('factor', 'dp')
The draws below stay inside these ranges and needn't reach their ends.
All inputs are finite; a program needn't handle non-finite values.
Results may differ from the reference program's by a relative error of at most 0.0069.
Values may be sent and summed in bfloat16 or wider, within the bound.
A program may use at most 64 MiB of HBM per device.

```python
import jax
import jax.numpy as jnp
from jax import lax

D = 8192
NB = 64
TOK_DEV = 1024
BLK = 128
HBLK = 512
TOKENS = 16384
N_DP = 16


def steps_of(stream_key, extent, cuts, low, high):
    def one(dim, blocks):
        steps = jax.random.uniform(jax.random.fold_in(jax.random.fold_in(stream_key, 6), dim), (blocks,), jnp.float32, low / len(cuts), high / len(cuts))
        return jnp.repeat(jnp.exp(steps), extent[dim] // blocks).reshape((-1,) + (1,) * (len(extent) - dim - 1))

    loudness = one(*cuts[0])
    for cut in cuts[1:]:
        loudness = loudness * one(*cut)
    return loudness


def scatter_about(stream_key, dims, spread, bound, split=(), held_as=jnp.bfloat16):
    drawn = spread * jax.random.normal(stream_key, dims, jnp.float32)
    if split:
        drawn = drawn * steps_of(stream_key, dims, split, -0.22, 0.18)
    return jnp.clip(drawn, -bound, bound).astype(held_as)


def setup_inputs(seed: int = 0) -> dict:
    keys = jax.random.split(jax.random.key(seed), 7)
    inputs = scatter_about(keys[0], (TOKENS, D), 1.0, 6.0, ((0, 16), (1, 16)))
    cotangent = scatter_about(keys[1], (TOKENS, D), 1.0, 6.0, ((0, 16), (1, 16)))
    first_factor = scatter_about(keys[2], (NB, BLK, BLK), BLK ** -0.5, 0.5, ((0, 16),))
    second_factor = scatter_about(keys[3], (NB, BLK, HBLK), BLK ** -0.5, 0.5, ((0, 16),))
    third_factor = scatter_about(keys[4], (NB, HBLK, BLK), HBLK ** -0.5, 0.25, ((0, 16),))
    fourth_factor = scatter_about(keys[5], (NB, BLK, BLK), BLK ** -0.5, 0.5, ((0, 16),))
    return {"inputs": inputs, "cotangent": cotangent, "first_factor": first_factor, "second_factor": second_factor, "third_factor": third_factor, "fourth_factor": fourth_factor}


def gelu_tanh(values):
    return jax.nn.gelu(values, approximate=True)

def widen(values):
    return values.astype(jnp.float32)

def permute_rows(values):
    count = values.shape[0]
    return jnp.transpose(values, (0, 2, 1)).reshape(count, NB, BLK)

def unpermute_rows(values):
    count = values.shape[0]
    return jnp.transpose(values.reshape(count, BLK, NB), (0, 2, 1))

def reference(inputs, cotangent, first_factor, second_factor, third_factor, fourth_factor):

    def group_step(carry, pieces):
        acc_one, acc_two, acc_three, acc_four = carry
        block_in, block_grad = pieces
        count = block_in.shape[0]
        tokens_in = block_in.reshape(count, NB, BLK)
        grad_out = block_grad.reshape(count, NB, BLK)
        first_out = jnp.einsum('tbi,bik->tbk', widen(tokens_in), widen(first_factor)).astype(jnp.bfloat16)
        mixed_one = permute_rows(first_out)
        pre_act = jnp.einsum('tcm,cmo->tco', widen(mixed_one), widen(second_factor))
        hidden = gelu_tanh(pre_act).astype(jnp.bfloat16)
        third_out = jnp.einsum('tco,cok->tck', widen(hidden), widen(third_factor)).astype(jnp.bfloat16)
        mixed_two = permute_rows(third_out)
        result = jnp.einsum('tcm,cmo->tco', widen(mixed_two), widen(fourth_factor)).astype(jnp.bfloat16)
        acc_four = acc_four + jnp.einsum('tcm,tco->cmo', widen(mixed_two), widen(grad_out))
        back_sent = jnp.einsum('tco,cmo->tcm', widen(grad_out), widen(fourth_factor)).astype(jnp.bfloat16)
        back_two = unpermute_rows(back_sent)
        acc_three = acc_three + jnp.einsum('tco,tck->cok', widen(hidden), widen(back_two))
        grad_hidden = jnp.einsum('tck,cok->tco', widen(back_two), widen(third_factor))
        grad_pre = jax.vjp(gelu_tanh, pre_act)[1](grad_hidden)[0].astype(jnp.bfloat16)
        acc_two = acc_two + jnp.einsum('tcm,tco->cmo', widen(mixed_one), widen(grad_pre))
        first_sent = jnp.einsum('tco,cmo->tcm', widen(grad_pre), widen(second_factor)).astype(jnp.bfloat16)
        back_one = unpermute_rows(first_sent)
        acc_one = acc_one + jnp.einsum('tbi,tbk->bik', widen(tokens_in), widen(back_one))
        input_grad = jnp.einsum('tbk,bik->tbi', widen(back_one), widen(first_factor)).astype(jnp.bfloat16)
        outputs = (result.reshape(count, D), input_grad.reshape(count, D))
        return ((acc_one, acc_two, acc_three, acc_four), outputs)
    start = (jnp.zeros((NB, BLK, BLK), jnp.float32), jnp.zeros((NB, BLK, HBLK), jnp.float32), jnp.zeros((NB, HBLK, BLK), jnp.float32), jnp.zeros((NB, BLK, BLK), jnp.float32))
    pieces = (inputs.reshape(N_DP, TOK_DEV, D), cotangent.reshape(N_DP, TOK_DEV, D))
    grads, outputs = lax.scan(group_step, start, pieces)
    result = outputs[0].reshape(TOKENS, D)
    input_grad = outputs[1].reshape(TOKENS, D)
    return (result, input_grad, grads[0], grads[1], grads[2], grads[3])
```

```python
import functools
import math

import jax
import jax.numpy as jnp
from jax import lax
from jax.experimental import pallas as pl
from jax.experimental.pallas import tpu as pltpu
from jax.sharding import PartitionSpec as P

BF = jnp.bfloat16
F32 = jnp.float32
CHUNKS = 4
SIDE = 4
HALF = 8
SCALE = math.sqrt(2.0 / math.pi)
CUBE = 0.044715


def nn(a, b):
    return lax.dot_general(a, b, (((1,), (0,)), ((), ())), preferred_element_type=F32)


def nt(a, b):
    return lax.dot_general(a, b, (((1,), (1,)), ((), ())), preferred_element_type=F32)


def tn(a, b):
    return lax.dot_general(a, b, (((0,), (0,)), ((), ())), preferred_element_type=F32)


def iotas(rows, cols, flip):
    axis = 1 if flip else 0
    shape = (cols, rows) if flip else (rows, cols)
    return (
        lax.broadcasted_iota(jnp.int32, shape, axis),
        lax.broadcasted_iota(jnp.int32, shape, 1 - axis),
    )


def one_hot(keep):
    return jnp.where(keep, 1.0, 0.0).astype(BF)


def pick_first(j, flip=False):
    row, k = iotas(512, 128, flip)
    return one_hot(
        (((row >> 2) & 3) == j) & (k == (row >> 5) * 8 + ((row >> 4) & 1) * 4 + (row & 3))
    )


def pick_second(half, flip=False):
    row, m = iotas(256, 128, flip)
    return one_hot((((row >> 1) & 1) == half) & (m == (row & 1) * 64 + (row >> 2)))


def pick_third(half, flip=False):
    row, k = iotas(256, 128, flip)
    return one_hot((((row >> 3) & 1) == half) & (k == (row >> 4) * 8 + (row & 7)))


def pick_fourth(c, flip=False):
    row, m = iotas(512, 128, flip)
    return one_hot(
        (((row >> 1) & 3) == c) & (m == (row & 1) * 64 + (row >> 5) * 4 + ((row >> 3) & 3))
    )


def kernel(
    x_hbm, cot_hbm, w1_hbm, w2_hbm, w3_hbm, w4_hbm,
    res_hbm, ig_hbm, g1_ref, g2_ref, g3_ref, g4_ref,
    x, cot, w1, w2, w3, w4,
    w1r, w4r, w2r, w2t, w3r, w3t,
    send_a, recv_a, send_b, recv_b, send_c, recv_c, send_d, recv_d,
    hidden, slope, grad_pre, res, ig,
    s1, s2, s3, s4,
    y_send, y_recv, z_send, z_recv, z_own,
    y4_send, y4_recv, z4_send, z4_recv, z4_own,
    t_send, t_recv,
    load_sem, store_sem, a2a_send, a2a_recv, rs_send, rs_recv,
):
    tokens = x.shape[1]
    me = lax.axis_index("factor")
    dp = lax.axis_index("dp")
    half, low = me // HALF, me % HALF
    row, col = dp // SIDE, dp % SIDE

    barrier = pltpu.get_barrier_semaphore()

    def greet(i, _):
        pl.semaphore_signal(barrier, inc=1, device_id={"factor": (me + i) % 16}, device_id_type=pl.DeviceIdType.MESH)
        pl.semaphore_signal(barrier, inc=1, device_id={"dp": (dp + i) % 16}, device_id_type=pl.DeviceIdType.MESH)
        return 0

    lax.fori_loop(1, 16, greet, 0)

    loads = []

    def load(src, dst):
        copy = pltpu.make_async_copy(src, dst, load_sem.at[len(loads)])
        copy.start()
        loads.append(copy)
        return copy

    got_w1 = load(w1_hbm, w1)
    got_x = [load(x_hbm.at[pl.ds(c * tokens, tokens)], x.at[c]) for c in range(CHUNKS)]
    got_w4 = load(w4_hbm, w4)
    got_cot = [load(cot_hbm.at[pl.ds(c * tokens, tokens)], cot.at[c]) for c in range(CHUNKS)]
    got_w2 = load(w2_hbm, w2)
    got_w3 = load(w3_hbm, w3)

    def spread(phase, c, send, recv):
        recv[c, me] = send[c, me]

        def one(peer):
            pltpu.make_async_remote_copy(
                src_ref=send.at[c, peer], dst_ref=recv.at[c, me],
                send_sem=a2a_send.at[phase, c], recv_sem=a2a_recv.at[phase, c],
                device_id={"factor": peer}, device_id_type=pl.DeviceIdType.MESH,
            ).start()

        def far(i, _):
            one((1 - half) * HALF + (low + i) % HALF)
            return 0

        def near(i, _):
            one(half * HALF + (low + i) % HALF)
            return 0

        lax.fori_loop(0, HALF, far, 0)
        lax.fori_loop(1, HALF, near, 0)

    def wait_bytes(ref, sem):
        pltpu.make_async_copy(ref, ref, sem).wait()

    def arrived(phase, c, recv):
        wait_bytes(recv.at[c, pl.ds(0, 15)], a2a_recv.at[phase, c])

    got_w1.wait()
    for j in range(4):
        w1r[:, j * 128 : (j + 1) * 128] = nt(pick_first(j), w1[j]).astype(BF)
    for c in range(CHUNKS):
        got_x[c].wait()
        send_a[c] = nt(w1r[...], x[c]).astype(BF).reshape(16, 32, tokens)
        if c == 0:
            pl.semaphore_wait(barrier, 30)
        spread(0, c, send_a, recv_a)

    got_w4.wait()
    for c in range(4):
        w4r[:, c * 128 : (c + 1) * 128] = nn(pick_fourth(c), w4[c]).astype(BF)
    for c in range(CHUNKS):
        got_cot[c].wait()
        send_b[c] = nt(w4r[...], cot[c]).astype(BF).reshape(16, 32, tokens)
        spread(1, c, send_b, recv_b)

    got_w2.wait()
    got_w3.wait()
    for p in range(2):
        for h in range(2):
            b = 2 * p + h
            w2r[p, :, h * 512 : (h + 1) * 512] = nn(pick_second(h), w2[b]).astype(BF)
            w2t[p, h * 512 : (h + 1) * 512, :] = tn(w2[b], pick_second(h, True)).astype(BF)
            w3r[p, h * 512 : (h + 1) * 512, :] = nn(w3[b], pick_third(h, True)).astype(BF)
            w3t[p, :, h * 512 : (h + 1) * 512] = nt(pick_third(h), w3[b]).astype(BF)
    s1[...] = jnp.zeros_like(s1)
    s2[...] = jnp.zeros_like(s2)
    s3[...] = jnp.zeros_like(s3)
    s4[...] = jnp.zeros_like(s4)

    def pair_rows(ref, c, p):
        return ref[c, :, pl.ds(p * 16, 16), :].reshape(256, tokens)

    def forward(c, _):
        arrived(0, c, recv_a)
        for p in range(2):
            mixed = pair_rows(recv_a, c, p)

            def tile(o, _):
                at = pl.ds(pl.multiple_of(o * 256, 256), 256)
                v = nn(w2t[p, at, :], mixed)
                sq = v * v
                t = jnp.tanh(v * (SCALE + (SCALE * CUBE) * sq))
                cdf = 0.5 + 0.5 * t
                hidden[c, p, at, :] = (v * cdf).astype(BF)
                slope[c, p, at, :] = cdf + (0.5 * v) * (1.0 - t * t) * (SCALE + (3.0 * SCALE * CUBE) * sq)
                return 0

            lax.fori_loop(0, 4, tile, 0)
            third = nn(w3t[p], hidden[c, p]).astype(BF)
            send_c[c, :, p * 16 : (p + 1) * 16, :] = third.reshape(16, 16, tokens)
        spread(2, c, send_c, recv_c)
        return 0

    lax.fori_loop(0, CHUNKS, forward, 0)

    def backward(c, _):
        arrived(1, c, recv_b)
        for p in range(2):
            back = pair_rows(recv_b, c, p)

            def tile(o, _):
                at = pl.ds(pl.multiple_of(o * 256, 256), 256)
                grad_pre[p, at, :] = (nn(w3r[p, at, :], back) * slope[c, p, at, :]).astype(BF)
                return 0

            lax.fori_loop(0, 4, tile, 0)
            first = nn(w2r[p], grad_pre[p]).astype(BF)
            send_d[c, :, p * 16 : (p + 1) * 16, :] = first.reshape(16, 16, tokens)
        spread(3, c, send_d, recv_d)
        for p in range(2):
            back = pair_rows(recv_b, c, p)
            mixed = pair_rows(recv_a, c, p)

            def sums(o, _):
                at = pl.ds(pl.multiple_of(o * 256, 256), 256)
                s3[p, at, :] += nt(hidden[c, p, at, :], back)
                s2[p, o] += nt(mixed, grad_pre[p, at, :])
                return 0

            lax.fori_loop(0, 4, sums, 0)
        return 0

    lax.fori_loop(0, CHUNKS, backward, 0)

    def scatter(n, axis, at, members, stride, base, send, recv):
        def one(i, _):
            peer = (at + i) % members
            pltpu.make_async_remote_copy(
                src_ref=send.at[peer], dst_ref=recv.at[at],
                send_sem=rs_send.at[n], recv_sem=rs_recv.at[n],
                device_id={"dp": base + peer * stride}, device_id_type=pl.DeviceIdType.MESH,
            ).start()
            return 0

        lax.fori_loop(1, members, one, 0)

    def scatter_y(n, send, recv):
        scatter(n, "y", row, SIDE, SIDE, col, send, recv)

    def scatter_z(n, send, recv):
        scatter(n, "z", col, SIDE, 1, row * SIDE, send, recv)

    for b in range(4):
        p, h = b // 2, b % 2
        third = s3[p, h * 512 : (h + 1) * 512, :].astype(BF)
        y_send[:, 1, :, b * 128 : (b + 1) * 128] = (
            nn(third, pick_third(h)).astype(BF).reshape(4, 128, 128)
        )
    for o in range(2):
        parts = [
            nn(pick_second(b % 2, True), s2[b // 2, 2 * (b % 2) + o].astype(BF)).reshape(16, 1, 8, 256)
            for b in range(4)
        ]
        y_send[:, 0, :, o * 256 : (o + 1) * 256] = (
            jnp.concatenate(parts, axis=1).reshape(4, 128, 256).astype(BF)
        )
    scatter_y(0, y_send, y_recv)

    def last_forward(c, _):
        arrived(2, c, recv_c)
        mixed = recv_c[c].reshape(512, tokens)
        res[c] = tn(mixed, w4r[...]).astype(BF)
        at = pl.ds(pl.multiple_of(c * tokens, tokens), tokens)
        pltpu.make_async_copy(res.at[c], res_hbm.at[at], store_sem.at[0, c]).start()
        s4[...] += nn(mixed, cot[c])
        return 0

    lax.fori_loop(0, CHUNKS, last_forward, 0)

    def own_rows(parts):
        return jnp.concatenate([v.reshape(16, 1, 8, 128) for v in parts], axis=1)

    parts = [nn(pick_fourth(c, True), s4[:, c * 128 : (c + 1) * 128].astype(BF)) for c in range(4)]
    y4_send[...] = own_rows(parts).reshape(4, 128, 128).astype(BF)
    scatter_y(1, y4_send, y4_recv)

    wait_bytes(y_recv.at[pl.ds(0, SIDE - 1)], rs_recv.at[0])
    for n in range(2):
        total = y_send[row, n].astype(F32)
        for i in range(1, SIDE):
            total += y_recv[(row + i) % SIDE, n].astype(F32)
        z_send[:, n] = total.astype(BF).reshape(SIDE, 32, 512)
        z_own[:, n] = total.reshape(SIDE, 32, 512)
    scatter_z(2, z_send, z_recv)

    def last_backward(c, _):
        arrived(3, c, recv_d)
        mixed = recv_d[c].reshape(512, tokens)
        ig[c] = tn(mixed, w1r[...]).astype(BF)
        at = pl.ds(pl.multiple_of(c * tokens, tokens), tokens)
        pltpu.make_async_copy(ig.at[c], ig_hbm.at[at], store_sem.at[1, c]).start()
        s1[...] += nn(mixed, x[c])
        return 0

    lax.fori_loop(0, CHUNKS - 1, last_backward, 0)

    wait_bytes(y4_recv.at[pl.ds(0, SIDE - 1)], rs_recv.at[1])
    total = y4_send[row].astype(F32)
    for i in range(1, SIDE):
        total += y4_recv[(row + i) % SIDE].astype(F32)
    z4_send[...] = total.astype(BF).reshape(SIDE, 32, 128)
    z4_own[...] = total.reshape(SIDE, 32, 128)
    scatter_z(3, z4_send, z4_recv)

    lax.fori_loop(CHUNKS - 1, CHUNKS, last_backward, 0)

    parts = [tn(s1[:, j * 128 : (j + 1) * 128].astype(BF), pick_first(j)) for j in range(4)]
    t_send[...] = own_rows(parts).reshape(16, 32, 128).astype(BF)
    scatter(4, "dp", dp, 16, 1, 0, t_send, t_recv)

    wait_bytes(z_recv.at[pl.ds(0, SIDE - 1)], rs_recv.at[2])
    total = z_own[col]
    for i in range(1, SIDE):
        total += z_recv[(col + i) % SIDE].astype(F32)
    g2_ref[...] = total[0].reshape(4, 8, 512)
    for j in range(4):
        g3_ref[j] = total[1, :, j * 128 : (j + 1) * 128]

    wait_bytes(z4_recv.at[pl.ds(0, SIDE - 1)], rs_recv.at[3])
    total = z4_own[col]
    for i in range(1, SIDE):
        total += z4_recv[(col + i) % SIDE].astype(F32)
    g4_ref[...] = total.reshape(4, 8, 128)

    wait_bytes(t_recv.at[pl.ds(0, 15)], rs_recv.at[4])
    total = t_send[dp].astype(F32)
    for i in range(1, 16):
        total += t_recv[(dp + i) % 16].astype(F32)
    g1_ref[...] = total.reshape(4, 8, 128)

    for c in range(CHUNKS):
        at = pl.ds(c * tokens, tokens)
        pltpu.make_async_copy(res.at[c], res_hbm.at[at], store_sem.at[0, c]).wait()
        pltpu.make_async_copy(ig.at[c], ig_hbm.at[at], store_sem.at[1, c]).wait()
        for phase, send in enumerate((send_a, send_b, send_c, send_d)):
            wait_bytes(send.at[c, pl.ds(0, 15)], a2a_send.at[phase, c])
    wait_bytes(y_send.at[pl.ds(0, SIDE - 1)], rs_send.at[0])
    wait_bytes(y4_send.at[pl.ds(0, SIDE - 1)], rs_send.at[1])
    wait_bytes(z_send.at[pl.ds(0, SIDE - 1)], rs_send.at[2])
    wait_bytes(z4_send.at[pl.ds(0, SIDE - 1)], rs_send.at[3])
    wait_bytes(t_send.at[pl.ds(0, 15)], rs_send.at[4])


def local(inputs, cotangent, first_factor, second_factor, third_factor, fourth_factor):
    count, width = inputs.shape
    tokens = count // CHUNKS
    any_spec = pl.BlockSpec(memory_space=pl.ANY)
    vmem = pl.BlockSpec(memory_space=pltpu.VMEM)
    packet = pltpu.VMEM((CHUNKS, 16, 32, tokens), BF)
    block = pltpu.VMEM((CHUNKS, tokens, width), BF)
    return pl.pallas_call(
        kernel,
        out_shape=(
            jax.ShapeDtypeStruct((count, width), BF),
            jax.ShapeDtypeStruct((count, width), BF),
            jax.ShapeDtypeStruct((4, 8, 128), F32),
            jax.ShapeDtypeStruct((4, 8, 512), F32),
            jax.ShapeDtypeStruct((4, 32, 128), F32),
            jax.ShapeDtypeStruct((4, 8, 128), F32),
        ),
        in_specs=[any_spec] * 6,
        out_specs=(any_spec, any_spec, vmem, vmem, vmem, vmem),
        scratch_shapes=[
            block, block,
            pltpu.VMEM((4, 128, 128), BF), pltpu.VMEM((4, 128, 512), BF),
            pltpu.VMEM((4, 512, 128), BF), pltpu.VMEM((4, 128, 128), BF),
            pltpu.VMEM((512, 512), BF), pltpu.VMEM((512, 512), BF),
            pltpu.VMEM((2, 256, 1024), BF), pltpu.VMEM((2, 1024, 256), BF),
            pltpu.VMEM((2, 1024, 256), BF), pltpu.VMEM((2, 256, 1024), BF),
            packet, packet, packet, packet, packet, packet, packet, packet,
            pltpu.VMEM((CHUNKS, 2, 1024, tokens), BF), pltpu.VMEM((CHUNKS, 2, 1024, tokens), F32),
            pltpu.VMEM((2, 1024, tokens), BF), block, block,
            pltpu.VMEM((512, 512), F32), pltpu.VMEM((2, 4, 256, 256), F32),
            pltpu.VMEM((2, 1024, 256), F32), pltpu.VMEM((512, 512), F32),
            pltpu.VMEM((SIDE, 2, 128, 512), BF), pltpu.VMEM((SIDE, 2, 128, 512), BF),
            pltpu.VMEM((SIDE, 2, 32, 512), BF), pltpu.VMEM((SIDE, 2, 32, 512), BF),
            pltpu.VMEM((SIDE, 2, 32, 512), F32),
            pltpu.VMEM((SIDE, 128, 128), BF), pltpu.VMEM((SIDE, 128, 128), BF),
            pltpu.VMEM((SIDE, 32, 128), BF), pltpu.VMEM((SIDE, 32, 128), BF),
            pltpu.VMEM((SIDE, 32, 128), F32),
            pltpu.VMEM((16, 32, 128), BF), pltpu.VMEM((16, 32, 128), BF),
            pltpu.SemaphoreType.DMA((2 * CHUNKS + 4,)), pltpu.SemaphoreType.DMA((2, CHUNKS)),
            pltpu.SemaphoreType.DMA((4, CHUNKS)), pltpu.SemaphoreType.DMA((4, CHUNKS)),
            pltpu.SemaphoreType.DMA((5,)), pltpu.SemaphoreType.DMA((5,)),
        ],
        compiler_params=pltpu.CompilerParams(
            collective_id=0, has_side_effects=True, vmem_limit_bytes=56 * 2**20
        ),
        cost_estimate=pl.CostEstimate(flops=8 * 10**9, bytes_accessed=6 * 10**6, transcendentals=2 * 10**6),
    )(inputs, cotangent, first_factor, second_factor, third_factor, fourth_factor)


def solution(mesh):
    in_specs = (
        P("dp", "factor"),
        P("dp", "factor"),
        P("factor", None, None),
        P("factor", None, None),
        P("factor", None, None),
        P("factor", None, None),
    )
    out_specs = (
        P("dp", "factor"),
        P("dp", "factor"),
        P("factor", "dp", None),
        P("factor", "dp", None),
        P("factor", "dp", None),
        P("factor", "dp", None),
    )
    return jax.shard_map(local, mesh=mesh, in_specs=in_specs, out_specs=out_specs, check_vma=False)
```

```python
import functools
import math

import jax
import jax.numpy as jnp
from jax import lax
from jax.experimental import pallas as pl
from jax.experimental.pallas import tpu as pltpu
from jax.sharding import PartitionSpec as P

BF = jnp.bfloat16
F32 = jnp.float32
CHUNKS = 4
SIDE = 4
HALF = 8
SCALE = math.sqrt(2.0 / math.pi)
CUBE = 0.044715


def nn(a, b):
    return lax.dot_general(a, b, (((1,), (0,)), ((), ())), preferred_element_type=F32)


def nt(a, b):
    return lax.dot_general(a, b, (((1,), (1,)), ((), ())), preferred_element_type=F32)


def tn(a, b):
    return lax.dot_general(a, b, (((0,), (0,)), ((), ())), preferred_element_type=F32)


def iotas(rows, cols, flip):
    axis = 1 if flip else 0
    shape = (cols, rows) if flip else (rows, cols)
    return (
        lax.broadcasted_iota(jnp.int32, shape, axis),
        lax.broadcasted_iota(jnp.int32, shape, 1 - axis),
    )


def one_hot(keep):
    return jnp.where(keep, 1.0, 0.0).astype(BF)


def pick_first(j, flip=False):
    row, k = iotas(512, 128, flip)
    return one_hot(
        (((row >> 2) & 3) == j) & (k == (row >> 5) * 8 + ((row >> 4) & 1) * 4 + (row & 3))
    )


def pick_second(half, flip=False):
    row, m = iotas(256, 128, flip)
    return one_hot((((row >> 1) & 1) == half) & (m == (row & 1) * 64 + (row >> 2)))


def pick_third(half, flip=False):
    row, k = iotas(256, 128, flip)
    return one_hot((((row >> 3) & 1) == half) & (k == (row >> 4) * 8 + (row & 7)))


def pick_fourth(c, flip=False):
    row, m = iotas(512, 128, flip)
    return one_hot(
        (((row >> 1) & 3) == c) & (m == (row & 1) * 64 + (row >> 5) * 4 + ((row >> 3) & 3))
    )


def kernel(
    x_hbm, cot_hbm, w1_hbm, w2_hbm, w3_hbm, w4_hbm,
    res_hbm, ig_hbm, g1_ref, g2_ref, g3_ref, g4_ref,
    x, cot, w1, w2, w3, w4,
    w1r, w4r, w2r, w2t, w3r, w3t,
    send_a, recv_a, send_b, recv_b, send_c, recv_c, send_d, recv_d,
    hidden, slope, grad_pre, res, ig,
    s1, s2, s3, s4,
    y_send, y_recv, z_send, z_recv, z_own,
    y4_send, y4_recv, z4_send, z4_recv, z4_own,
    y1_send, y1_recv, z1_send, z1_recv, z1_own,
    load_sem, store_sem, a2a_send, a2a_recv, rs_send, rs_recv,
):
    tokens = x.shape[1]
    me = lax.axis_index("factor")
    dp = lax.axis_index("dp")
    half, low = me // HALF, me % HALF
    row, col = dp // SIDE, dp % SIDE

    barrier = pltpu.get_barrier_semaphore()

    def greet(i, _):
        for peer in ({"factor": (me + i) % 16}, {"dp": (dp + i) % 16}):
            pl.semaphore_signal(barrier, inc=1, device_id=peer, device_id_type=pl.DeviceIdType.MESH)
        return 0

    lax.fori_loop(1, 16, greet, 0)

    loads = []

    def load(src, dst):
        copy = pltpu.make_async_copy(src, dst, load_sem.at[len(loads)])
        copy.start()
        loads.append(copy)
        return copy

    got_w1 = load(w1_hbm, w1)
    got_x = [load(x_hbm.at[pl.ds(c * tokens, tokens)], x.at[c]) for c in range(CHUNKS)]
    got_w4 = load(w4_hbm, w4)
    got_cot = [load(cot_hbm.at[pl.ds(c * tokens, tokens)], cot.at[c]) for c in range(CHUNKS)]
    got_w2 = load(w2_hbm, w2)
    got_w3 = load(w3_hbm, w3)

    def spread(phase, c, send, recv):
        recv[c, me] = send[c, me]

        def one(peer):
            pltpu.make_async_remote_copy(
                src_ref=send.at[c, peer], dst_ref=recv.at[c, me],
                send_sem=a2a_send.at[phase, c], recv_sem=a2a_recv.at[phase, c],
                device_id={"factor": peer}, device_id_type=pl.DeviceIdType.MESH,
            ).start()

        def far(i, _):
            one((1 - half) * HALF + (low + i) % HALF)
            return 0

        def near(i, _):
            one(half * HALF + (low + i) % HALF)
            return 0

        lax.fori_loop(0, HALF, far, 0)
        lax.fori_loop(1, HALF, near, 0)

    def wait_bytes(ref, sem):
        pltpu.make_async_copy(ref, ref, sem).wait()

    def arrived(phase, c, recv):
        wait_bytes(recv.at[c, pl.ds(0, 15)], a2a_recv.at[phase, c])

    got_w1.wait()
    for j in range(4):
        w1r[:, j * 128 : (j + 1) * 128] = nt(pick_first(j), w1[j]).astype(BF)
    for c in range(CHUNKS):
        got_x[c].wait()
        send_a[c] = nt(w1r[...], x[c]).astype(BF).reshape(16, 32, tokens)
        if c == 0:
            pl.semaphore_wait(barrier, 30)
        spread(0, c, send_a, recv_a)

    got_w4.wait()
    for c in range(4):
        w4r[:, c * 128 : (c + 1) * 128] = nn(pick_fourth(c), w4[c]).astype(BF)
    for c in range(CHUNKS):
        got_cot[c].wait()
        send_b[c] = nt(w4r[...], cot[c]).astype(BF).reshape(16, 32, tokens)
        spread(1, c, send_b, recv_b)

    got_w2.wait()
    got_w3.wait()
    for p in range(2):
        for h in range(2):
            b = 2 * p + h
            w2r[p, :, h * 512 : (h + 1) * 512] = nn(pick_second(h), w2[b]).astype(BF)
            w2t[p, h * 512 : (h + 1) * 512, :] = tn(w2[b], pick_second(h, True)).astype(BF)
            w3r[p, h * 512 : (h + 1) * 512, :] = nn(w3[b], pick_third(h, True)).astype(BF)
            w3t[p, :, h * 512 : (h + 1) * 512] = nt(pick_third(h), w3[b]).astype(BF)
    s1[...] = jnp.zeros_like(s1)
    s2[...] = jnp.zeros_like(s2)
    s3[...] = jnp.zeros_like(s3)
    s4[...] = jnp.zeros_like(s4)

    def pair_rows(ref, c, p):
        return ref[c, :, pl.ds(p * 16, 16), :].reshape(256, tokens)

    def forward(c, _):
        arrived(0, c, recv_a)
        for p in range(2):
            mixed = pair_rows(recv_a, c, p)

            def tile(o, _):
                at = pl.ds(pl.multiple_of(o * 256, 256), 256)
                v = nn(w2t[p, at, :], mixed)
                sq = v * v
                t = jnp.tanh(v * (SCALE + (SCALE * CUBE) * sq))
                cdf = 0.5 + 0.5 * t
                hidden[c, p, at, :] = (v * cdf).astype(BF)
                slope[c, p, at, :] = cdf + (0.5 * v) * (1.0 - t * t) * (SCALE + (3.0 * SCALE * CUBE) * sq)
                return 0

            lax.fori_loop(0, 4, tile, 0)
            third = nn(w3t[p], hidden[c, p]).astype(BF)
            send_c[c, :, p * 16 : (p + 1) * 16, :] = third.reshape(16, 16, tokens)
        spread(2, c, send_c, recv_c)
        return 0

    lax.fori_loop(0, CHUNKS, forward, 0)

    def backward(c, _):
        arrived(1, c, recv_b)
        for p in range(2):
            back = pair_rows(recv_b, c, p)

            def tile(o, _):
                at = pl.ds(pl.multiple_of(o * 256, 256), 256)
                grad_pre[p, at, :] = (nn(w3r[p, at, :], back) * slope[c, p, at, :]).astype(BF)
                return 0

            lax.fori_loop(0, 4, tile, 0)
            first = nn(w2r[p], grad_pre[p]).astype(BF)
            send_d[c, :, p * 16 : (p + 1) * 16, :] = first.reshape(16, 16, tokens)
        spread(3, c, send_d, recv_d)
        for p in range(2):
            back = pair_rows(recv_b, c, p)
            mixed = pair_rows(recv_a, c, p)

            def sums(o, _):
                at = pl.ds(pl.multiple_of(o * 256, 256), 256)
                s3[p, at, :] += nt(hidden[c, p, at, :], back)
                s2[p, o] += nt(mixed, grad_pre[p, at, :])
                return 0

            lax.fori_loop(0, 4, sums, 0)
        return 0

    lax.fori_loop(0, CHUNKS, backward, 0)

    def scatter(n, at, members, stride, base, send, recv):
        def one(i, _):
            peer = (at + i) % members
            pltpu.make_async_remote_copy(
                src_ref=send.at[peer], dst_ref=recv.at[at],
                send_sem=rs_send.at[n], recv_sem=rs_recv.at[n],
                device_id={"dp": base + peer * stride}, device_id_type=pl.DeviceIdType.MESH,
            ).start()
            return 0

        lax.fori_loop(1, members, one, 0)

    def scatter_y(n, send, recv):
        scatter(n, row, SIDE, SIDE, col, send, recv)

    def scatter_z(n, send, recv):
        scatter(n, col, SIDE, 1, row * SIDE, send, recv)

    for b in range(4):
        p, h = b // 2, b % 2
        third = s3[p, h * 512 : (h + 1) * 512, :].astype(BF)
        y_send[:, 1, :, b * 128 : (b + 1) * 128] = (
            nn(third, pick_third(h)).astype(BF).reshape(4, 128, 128)
        )
    for o in range(2):
        parts = [
            nn(pick_second(b % 2, True), s2[b // 2, 2 * (b % 2) + o].astype(BF)).reshape(16, 1, 8, 256)
            for b in range(4)
        ]
        y_send[:, 0, :, o * 256 : (o + 1) * 256] = (
            jnp.concatenate(parts, axis=1).reshape(4, 128, 256).astype(BF)
        )
    scatter_y(0, y_send, y_recv)

    def last_forward(c, _):
        arrived(2, c, recv_c)
        mixed = recv_c[c].reshape(512, tokens)
        res[c] = tn(mixed, w4r[...]).astype(BF)
        at = pl.ds(pl.multiple_of(c * tokens, tokens), tokens)
        pltpu.make_async_copy(res.at[c], res_hbm.at[at], store_sem.at[0, c]).start()
        s4[...] += nn(mixed, cot[c])
        return 0

    lax.fori_loop(0, CHUNKS, last_forward, 0)

    def own_rows(parts):
        return jnp.concatenate([v.reshape(16, 1, 8, 128) for v in parts], axis=1)

    parts = [nn(pick_fourth(c, True), s4[:, c * 128 : (c + 1) * 128].astype(BF)) for c in range(4)]
    y4_send[...] = own_rows(parts).reshape(4, 128, 128).astype(BF)
    scatter_y(1, y4_send, y4_recv)

    wait_bytes(y_recv.at[pl.ds(0, SIDE - 1)], rs_recv.at[0])
    for n in range(2):
        total = y_send[row, n].astype(F32)
        for i in range(1, SIDE):
            total += y_recv[(row + i) % SIDE, n].astype(F32)
        z_send[n] = total.astype(BF).reshape(SIDE, 32, 512)
        z_own[n] = total.reshape(SIDE, 32, 512)

    def input_rows(c):
        ig[c] = tn(recv_d[c].reshape(512, tokens), w1r[...]).astype(BF)
        at = pl.ds(pl.multiple_of(c * tokens, tokens), tokens)
        pltpu.make_async_copy(ig.at[c], ig_hbm.at[at], store_sem.at[1, c]).start()

    def last_backward(c, _):
        arrived(3, c, recv_d)
        s1[...] += nn(recv_d[c].reshape(512, tokens), x[c])
        input_rows(c)
        return 0

    lax.fori_loop(0, CHUNKS - 1, last_backward, 0)

    def fold(n, y_out, y_in, z_out, own):
        wait_bytes(y_in.at[pl.ds(0, SIDE - 1)], rs_recv.at[n])
        total = y_out[row].astype(F32)
        for i in range(1, SIDE):
            total += y_in[(row + i) % SIDE].astype(F32)
        z_out[...] = total.astype(BF).reshape(SIDE, 32, 128)
        own[...] = total.reshape(SIDE, 32, 128)

    fold(1, y4_send, y4_recv, z4_send, z4_own)

    arrived(3, CHUNKS - 1, recv_d)
    scatter_z(2, z_send.at[0], z_recv.at[0])
    scatter_z(5, z_send.at[1], z_recv.at[1])
    scatter_z(3, z4_send, z4_recv)
    s1[...] += nn(recv_d[CHUNKS - 1].reshape(512, tokens), x[CHUNKS - 1])
    parts = [tn(s1[:, j * 128 : (j + 1) * 128].astype(BF), pick_first(j)) for j in range(4)]
    y1_send[...] = own_rows(parts).reshape(4, 128, 128).astype(BF)
    scatter_y(4, y1_send, y1_recv)
    input_rows(CHUNKS - 1)
    fold(4, y1_send, y1_recv, z1_send, z1_own)
    scatter_z(6, z1_send, z1_recv)

    for n in range(2):
        wait_bytes(z_recv.at[n, pl.ds(0, SIDE - 1)], rs_recv.at[(2, 5)[n]])
        total = z_own[n, col]
        for i in range(1, SIDE):
            total += z_recv[n, (col + i) % SIDE].astype(F32)
        if n == 0:
            g2_ref[...] = total.reshape(4, 8, 512)
        else:
            for j in range(4):
                g3_ref[j] = total[:, j * 128 : (j + 1) * 128]

    for n, own, recv, out in ((3, z4_own, z4_recv, g4_ref), (6, z1_own, z1_recv, g1_ref)):
        wait_bytes(recv.at[pl.ds(0, SIDE - 1)], rs_recv.at[n])
        total = own[col]
        for i in range(1, SIDE):
            total += recv[(col + i) % SIDE].astype(F32)
        out[...] = total.reshape(4, 8, 128)

    for c in range(CHUNKS):
        at = pl.ds(c * tokens, tokens)
        pltpu.make_async_copy(res.at[c], res_hbm.at[at], store_sem.at[0, c]).wait()
        pltpu.make_async_copy(ig.at[c], ig_hbm.at[at], store_sem.at[1, c]).wait()
        for phase, send in enumerate((send_a, send_b, send_c, send_d)):
            wait_bytes(send.at[c, pl.ds(0, 15)], a2a_send.at[phase, c])
    wait_bytes(y_send.at[pl.ds(0, SIDE - 1)], rs_send.at[0])
    wait_bytes(y4_send.at[pl.ds(0, SIDE - 1)], rs_send.at[1])
    wait_bytes(z_send.at[0, pl.ds(0, SIDE - 1)], rs_send.at[2])
    wait_bytes(z_send.at[1, pl.ds(0, SIDE - 1)], rs_send.at[5])
    wait_bytes(z4_send.at[pl.ds(0, SIDE - 1)], rs_send.at[3])
    wait_bytes(y1_send.at[pl.ds(0, SIDE - 1)], rs_send.at[4])
    wait_bytes(z1_send.at[pl.ds(0, SIDE - 1)], rs_send.at[6])


def publish(*refs):
    sources, targets, held, sem = refs[:6], refs[6:12], refs[12:18], refs[18]
    copies = []
    for n, (source, target, slot) in enumerate(zip(sources, targets, held)):
        parts = CHUNKS if n < 2 else 1
        rows = source.shape[0] // parts
        for i in range(parts):
            at = pl.ds(i * rows, rows)
            k = len(copies)
            copies.append((
                pltpu.make_async_copy(source.at[at], slot.at[at], sem.at[0, k]),
                pltpu.make_async_copy(slot.at[at], target.at[at], sem.at[1, k]),
            ))
    for come, _ in copies:
        come.start()
    for come, go in copies:
        come.wait()
        go.start()
    for _, go in copies:
        go.wait()


def local(inputs, cotangent, first_factor, second_factor, third_factor, fourth_factor):
    count, width = inputs.shape
    tokens = count // CHUNKS
    any_spec = pl.BlockSpec(memory_space=pl.ANY)
    vmem = pl.BlockSpec(memory_space=pltpu.VMEM)
    packet = pltpu.VMEM((CHUNKS, 16, 32, tokens), BF)
    block = pltpu.VMEM((CHUNKS, tokens, width), BF)
    outs = (
        jax.ShapeDtypeStruct((count, width), BF),
        jax.ShapeDtypeStruct((count, width), BF),
        jax.ShapeDtypeStruct((4, 8, 128), F32),
        jax.ShapeDtypeStruct((4, 8, 512), F32),
        jax.ShapeDtypeStruct((4, 32, 128), F32),
        jax.ShapeDtypeStruct((4, 8, 128), F32),
    )
    made = pl.pallas_call(
        kernel,
        out_shape=outs,
        in_specs=[any_spec] * 6,
        out_specs=(any_spec, any_spec, vmem, vmem, vmem, vmem),
        scratch_shapes=[
            block, block,
            pltpu.VMEM((4, 128, 128), BF), pltpu.VMEM((4, 128, 512), BF),
            pltpu.VMEM((4, 512, 128), BF), pltpu.VMEM((4, 128, 128), BF),
            pltpu.VMEM((512, 512), BF), pltpu.VMEM((512, 512), BF),
            pltpu.VMEM((2, 256, 1024), BF), pltpu.VMEM((2, 1024, 256), BF),
            pltpu.VMEM((2, 1024, 256), BF), pltpu.VMEM((2, 256, 1024), BF),
            packet, packet, packet, packet, packet, packet, packet, packet,
            pltpu.VMEM((CHUNKS, 2, 1024, tokens), BF), pltpu.VMEM((CHUNKS, 2, 1024, tokens), F32),
            pltpu.VMEM((2, 1024, tokens), BF), block, block,
            pltpu.VMEM((512, 512), F32), pltpu.VMEM((2, 4, 256, 256), F32),
            pltpu.VMEM((2, 1024, 256), F32), pltpu.VMEM((512, 512), F32),
            pltpu.VMEM((SIDE, 2, 128, 512), BF), pltpu.VMEM((SIDE, 2, 128, 512), BF),
            pltpu.VMEM((2, SIDE, 32, 512), BF), pltpu.VMEM((2, SIDE, 32, 512), BF),
            pltpu.VMEM((2, SIDE, 32, 512), F32),
            pltpu.VMEM((SIDE, 128, 128), BF), pltpu.VMEM((SIDE, 128, 128), BF),
            pltpu.VMEM((SIDE, 32, 128), BF), pltpu.VMEM((SIDE, 32, 128), BF),
            pltpu.VMEM((SIDE, 32, 128), F32),
            pltpu.VMEM((SIDE, 128, 128), BF), pltpu.VMEM((SIDE, 128, 128), BF),
            pltpu.VMEM((SIDE, 32, 128), BF), pltpu.VMEM((SIDE, 32, 128), BF),
            pltpu.VMEM((SIDE, 32, 128), F32),
            pltpu.SemaphoreType.DMA((2 * CHUNKS + 4,)), pltpu.SemaphoreType.DMA((2, CHUNKS)),
            pltpu.SemaphoreType.DMA((4, CHUNKS)), pltpu.SemaphoreType.DMA((4, CHUNKS)),
            pltpu.SemaphoreType.DMA((7,)), pltpu.SemaphoreType.DMA((7,)),
        ],
        compiler_params=pltpu.CompilerParams(
            collective_id=0, has_side_effects=True, vmem_limit_bytes=56 * 2**20
        ),
        cost_estimate=pl.CostEstimate(flops=8 * 10**9, bytes_accessed=6 * 10**6, transcendentals=2 * 10**6),
    )(inputs, cotangent, first_factor, second_factor, third_factor, fourth_factor)
    return pl.pallas_call(
        publish,
        out_shape=outs,
        in_specs=[any_spec] * 6,
        out_specs=(any_spec,) * 6,
        scratch_shapes=[pltpu.VMEM(out.shape, out.dtype) for out in outs]
        + [pltpu.SemaphoreType.DMA((2, 2 * CHUNKS + 4))],
        cost_estimate=pl.CostEstimate(flops=0, bytes_accessed=5 * 10**6, transcendentals=0),
    )(*made)


def solution(mesh):
    in_specs = (
        P("dp", "factor"),
        P("dp", "factor"),
        P("factor", None, None),
        P("factor", None, None),
        P("factor", None, None),
        P("factor", None, None),
    )
    out_specs = (
        P("dp", "factor"),
        P("dp", "factor"),
        P("factor", "dp", None),
        P("factor", "dp", None),
        P("factor", "dp", None),
        P("factor", "dp", None),
    )
    return jax.shard_map(local, mesh=mesh, in_specs=in_specs, out_specs=out_specs, check_vma=False)
```

```python
import functools
import math

import jax
import jax.numpy as jnp
from jax import lax
from jax.experimental import pallas as pl
from jax.experimental.pallas import tpu as pltpu
from jax.sharding import PartitionSpec as P

BF = jnp.bfloat16
F32 = jnp.float32
CHUNKS = 2
SIDE = 4
HALF = 8
SCALE = math.sqrt(2.0 / math.pi)
CUBE = 0.044715


def nn(a, b):
    return lax.dot_general(a, b, (((1,), (0,)), ((), ())), preferred_element_type=F32)


def nt(a, b):
    return lax.dot_general(a, b, (((1,), (1,)), ((), ())), preferred_element_type=F32)


def tn(a, b):
    return lax.dot_general(a, b, (((0,), (0,)), ((), ())), preferred_element_type=F32)


def iotas(rows, cols, flip):
    axis = 1 if flip else 0
    shape = (cols, rows) if flip else (rows, cols)
    return (
        lax.broadcasted_iota(jnp.int32, shape, axis),
        lax.broadcasted_iota(jnp.int32, shape, 1 - axis),
    )


def one_hot(keep):
    return jnp.where(keep, 1.0, 0.0).astype(BF)


def pick_first(j, flip=False):
    row, k = iotas(512, 128, flip)
    return one_hot(
        (((row >> 2) & 3) == j) & (k == (row >> 5) * 8 + ((row >> 4) & 1) * 4 + (row & 3))
    )


def pick_second(half, flip=False):
    row, m = iotas(256, 128, flip)
    return one_hot((((row >> 1) & 1) == half) & (m == (row & 1) * 64 + (row >> 2)))


def pick_third(half, flip=False):
    row, k = iotas(256, 128, flip)
    return one_hot((((row >> 3) & 1) == half) & (k == (row >> 4) * 8 + (row & 7)))


def pick_fourth(c, flip=False):
    row, m = iotas(512, 128, flip)
    return one_hot(
        (((row >> 1) & 3) == c) & (m == (row & 1) * 64 + (row >> 5) * 4 + ((row >> 3) & 3))
    )


def kernel(
    x_hbm, cot_hbm, w1_hbm, w2_hbm, w3_hbm, w4_hbm,
    res_hbm, ig_hbm, g1_ref, g2_ref, g3_ref, g4_ref,
    x, cot, w1, w2, w3, w4,
    w1r, w4r, w2r, w2t, w3r, w3t,
    send_a, recv_a, send_b, recv_b, send_c, recv_c, send_d, recv_d,
    hidden, slope, grad_pre, res, ig,
    s1, s2, s3, s4,
    y_send, y_recv, z_send, z_recv, z_own,
    y4_send, y4_recv, z4_send, z4_recv, z4_own,
    y1_send, y1_recv, z1_send, z1_recv, z1_own,
    load_sem, store_sem, a2a_send, a2a_recv, rs_send, rs_recv,
):
    tokens = x.shape[1]
    me = lax.axis_index("factor")
    dp = lax.axis_index("dp")
    half, low = me // HALF, me % HALF
    row, col = dp // SIDE, dp % SIDE

    barrier = pltpu.get_barrier_semaphore()

    loads = []

    def load(src, dst):
        copy = pltpu.make_async_copy(src, dst, load_sem.at[len(loads)])
        copy.start()
        loads.append(copy)
        return copy

    def load_rows(src, dst, c):
        return load(src.at[pl.ds(c * tokens, tokens)], dst.at[c])

    got_w1 = load(w1_hbm, w1)
    got_x = [load_rows(x_hbm, x, 0)]

    def greet(i, _):
        pl.semaphore_signal(barrier, inc=1, device_id={"factor": (me + i) % 16}, device_id_type=pl.DeviceIdType.MESH)
        return 0

    def greet_dp(i, _):
        for group in ((row + i) % SIDE * SIDE + col, row * SIDE + (col + i) % SIDE):
            pl.semaphore_signal(barrier, inc=1, device_id={"dp": group}, device_id_type=pl.DeviceIdType.MESH)
        return 0

    lax.fori_loop(1, 16, greet, 0)
    lax.fori_loop(1, SIDE, greet_dp, 0)

    def spread(phase, c, send, recv):
        recv[c, me] = send[c, me]

        def one(peer):
            pltpu.make_async_remote_copy(
                src_ref=send.at[c, peer], dst_ref=recv.at[c, me],
                send_sem=a2a_send.at[phase, c], recv_sem=a2a_recv.at[phase, c],
                device_id={"factor": peer}, device_id_type=pl.DeviceIdType.MESH,
            ).start()

        def far(i, _):
            one((1 - half) * HALF + (low + i) % HALF)
            return 0

        def near(i, _):
            one(half * HALF + (low + i) % HALF)
            return 0

        lax.fori_loop(0, HALF, far, 0)
        lax.fori_loop(1, HALF, near, 0)

    def wait_bytes(ref, sem):
        pltpu.make_async_copy(ref, ref, sem).wait()

    def arrived(phase, c, recv):
        wait_bytes(recv.at[c, pl.ds(0, 15)], a2a_recv.at[phase, c])

    got_w1.wait()
    for j in range(4):
        w1r[:, j * 128 : (j + 1) * 128] = nt(pick_first(j), w1[j]).astype(BF)
    for c in range(CHUNKS):
        got_x[c].wait()
        if c == 0:
            got_x += [load_rows(x_hbm, x, n) for n in range(1, CHUNKS)]
            got_w4 = load(w4_hbm, w4)
            got_cot = [load_rows(cot_hbm, cot, n) for n in range(CHUNKS)]
            got_w2 = load(w2_hbm, w2)
            got_w3 = load(w3_hbm, w3)
        send_a[c] = nt(w1r[...], x[c]).astype(BF).reshape(16, 32, tokens)
        if c == 0:
            pl.semaphore_wait(barrier, 15 + 2 * (SIDE - 1))
        spread(0, c, send_a, recv_a)

    got_w4.wait()
    for c in range(4):
        w4r[:, c * 128 : (c + 1) * 128] = nn(pick_fourth(c), w4[c]).astype(BF)
    for c in range(CHUNKS):
        got_cot[c].wait()
        send_b[c] = nt(w4r[...], cot[c]).astype(BF).reshape(16, 32, tokens)
        spread(1, c, send_b, recv_b)

    got_w2.wait()
    got_w3.wait()
    for p in range(2):
        for h in range(2):
            b = 2 * p + h
            w2r[p, :, h * 512 : (h + 1) * 512] = nn(pick_second(h), w2[b]).astype(BF)
            w2t[p, h * 512 : (h + 1) * 512, :] = tn(w2[b], pick_second(h, True)).astype(BF)
            w3r[p, h * 512 : (h + 1) * 512, :] = nn(w3[b], pick_third(h, True)).astype(BF)
            w3t[p, :, h * 512 : (h + 1) * 512] = nt(pick_third(h), w3[b]).astype(BF)
    s1[...] = jnp.zeros_like(s1)
    s2[...] = jnp.zeros_like(s2)
    s3[...] = jnp.zeros_like(s3)
    s4[...] = jnp.zeros_like(s4)

    def pair_rows(ref, c, p):
        return ref[c, :, pl.ds(p * 16, 16), :].reshape(256, tokens)

    def forward(c, _):
        arrived(0, c, recv_a)
        for p in range(2):
            mixed = pair_rows(recv_a, c, p)

            def tile(o, _):
                at = pl.ds(pl.multiple_of(o * 256, 256), 256)
                v = nn(w2t[p, at, :], mixed)
                sq = v * v
                t = jnp.tanh(v * (SCALE + (SCALE * CUBE) * sq))
                cdf = 0.5 + 0.5 * t
                hidden[c, p, at, :] = (v * cdf).astype(BF)
                slope[c, p, at, :] = cdf + (0.5 * v) * (1.0 - t * t) * (SCALE + (3.0 * SCALE * CUBE) * sq)
                return 0

            lax.fori_loop(0, 4, tile, 0)
            third = nn(w3t[p], hidden[c, p]).astype(BF)
            send_c[c, :, p * 16 : (p + 1) * 16, :] = third.reshape(16, 16, tokens)
        spread(2, c, send_c, recv_c)
        return 0

    lax.fori_loop(0, CHUNKS, forward, 0)

    def backward(c, _):
        arrived(1, c, recv_b)
        for p in range(2):
            back = pair_rows(recv_b, c, p)

            def tile(o, _):
                at = pl.ds(pl.multiple_of(o * 256, 256), 256)
                grad_pre[p, at, :] = (nn(w3r[p, at, :], back) * slope[c, p, at, :]).astype(BF)
                return 0

            lax.fori_loop(0, 4, tile, 0)
            first = nn(w2r[p], grad_pre[p]).astype(BF)
            send_d[c, :, p * 16 : (p + 1) * 16, :] = first.reshape(16, 16, tokens)
        spread(3, c, send_d, recv_d)
        for p in range(2):
            back = pair_rows(recv_b, c, p)
            mixed = pair_rows(recv_a, c, p)

            def sums(o, _):
                at = pl.ds(pl.multiple_of(o * 256, 256), 256)
                s3[p, at, :] += nt(hidden[c, p, at, :], back)
                s2[p, o] += nt(mixed, grad_pre[p, at, :])
                return 0

            lax.fori_loop(0, 4, sums, 0)
        return 0

    lax.fori_loop(0, CHUNKS, backward, 0)

    def scatter(n, at, members, stride, base, send, recv):
        def one(i, _):
            peer = (at + i) % members
            pltpu.make_async_remote_copy(
                src_ref=send.at[peer], dst_ref=recv.at[at],
                send_sem=rs_send.at[n], recv_sem=rs_recv.at[n],
                device_id={"dp": base + peer * stride}, device_id_type=pl.DeviceIdType.MESH,
            ).start()
            return 0

        lax.fori_loop(1, members, one, 0)

    def scatter_y(n, send, recv):
        scatter(n, row, SIDE, SIDE, col, send, recv)

    def scatter_z(n, send, recv):
        scatter(n, col, SIDE, 1, row * SIDE, send, recv)

    for b in range(4):
        p, h = b // 2, b % 2
        third = s3[p, h * 512 : (h + 1) * 512, :].astype(BF)
        y_send[:, 1, :, b * 128 : (b + 1) * 128] = (
            nn(third, pick_third(h)).astype(BF).reshape(4, 128, 128)
        )
    for o in range(2):
        parts = [
            nn(pick_second(b % 2, True), s2[b // 2, 2 * (b % 2) + o].astype(BF)).reshape(16, 1, 8, 256)
            for b in range(4)
        ]
        y_send[:, 0, :, o * 256 : (o + 1) * 256] = (
            jnp.concatenate(parts, axis=1).reshape(4, 128, 256).astype(BF)
        )
    scatter_y(0, y_send, y_recv)

    def last_forward(c, _):
        arrived(2, c, recv_c)
        mixed = recv_c[c].reshape(512, tokens)
        res[c] = tn(mixed, w4r[...]).astype(BF)
        at = pl.ds(pl.multiple_of(c * tokens, tokens), tokens)
        pltpu.make_async_copy(res.at[c], res_hbm.at[at], store_sem.at[0, c]).start()
        s4[...] += nn(mixed, cot[c])
        return 0

    lax.fori_loop(0, CHUNKS, last_forward, 0)

    def own_rows(parts):
        return jnp.concatenate([v.reshape(16, 1, 8, 128) for v in parts], axis=1)

    parts = [nn(pick_fourth(c, True), s4[:, c * 128 : (c + 1) * 128].astype(BF)) for c in range(4)]
    y4_send[...] = own_rows(parts).reshape(4, 128, 128).astype(BF)
    scatter_y(1, y4_send, y4_recv)

    wait_bytes(y_recv.at[pl.ds(0, SIDE - 1)], rs_recv.at[0])
    for n in range(2):
        total = y_send[row, n].astype(F32)
        for i in range(1, SIDE):
            total += y_recv[(row + i) % SIDE, n].astype(F32)
        z_send[n] = total.astype(BF).reshape(SIDE, 32, 512)
        z_own[n] = total.reshape(SIDE, 32, 512)

    def input_rows(c):
        ig[c] = tn(recv_d[c].reshape(512, tokens), w1r[...]).astype(BF)
        at = pl.ds(pl.multiple_of(c * tokens, tokens), tokens)
        pltpu.make_async_copy(ig.at[c], ig_hbm.at[at], store_sem.at[1, c]).start()

    def last_backward(c, _):
        arrived(3, c, recv_d)
        s1[...] += nn(recv_d[c].reshape(512, tokens), x[c])
        input_rows(c)
        return 0

    lax.fori_loop(0, CHUNKS - 1, last_backward, 0)

    def fold(n, y_out, y_in, z_out, own):
        wait_bytes(y_in.at[pl.ds(0, SIDE - 1)], rs_recv.at[n])
        total = y_out[row].astype(F32)
        for i in range(1, SIDE):
            total += y_in[(row + i) % SIDE].astype(F32)
        z_out[...] = total.astype(BF).reshape(SIDE, 32, 128)
        own[...] = total.reshape(SIDE, 32, 128)

    fold(1, y4_send, y4_recv, z4_send, z4_own)

    arrived(3, CHUNKS - 1, recv_d)
    scatter_z(2, z_send.at[0], z_recv.at[0])
    scatter_z(5, z_send.at[1], z_recv.at[1])
    scatter_z(3, z4_send, z4_recv)
    s1[...] += nn(recv_d[CHUNKS - 1].reshape(512, tokens), x[CHUNKS - 1])
    parts = [tn(s1[:, j * 128 : (j + 1) * 128].astype(BF), pick_first(j)) for j in range(4)]
    y1_send[...] = own_rows(parts).reshape(4, 128, 128).astype(BF)
    scatter_y(4, y1_send, y1_recv)
    input_rows(CHUNKS - 1)
    fold(4, y1_send, y1_recv, z1_send, z1_own)
    scatter_z(6, z1_send, z1_recv)

    for n in range(2):
        wait_bytes(z_recv.at[n, pl.ds(0, SIDE - 1)], rs_recv.at[(2, 5)[n]])
        total = z_own[n, col]
        for i in range(1, SIDE):
            total += z_recv[n, (col + i) % SIDE].astype(F32)
        if n == 0:
            g2_ref[...] = total.reshape(4, 8, 512)
        else:
            for j in range(4):
                g3_ref[j] = total[:, j * 128 : (j + 1) * 128]

    for n, own, recv, out in ((3, z4_own, z4_recv, g4_ref), (6, z1_own, z1_recv, g1_ref)):
        wait_bytes(recv.at[pl.ds(0, SIDE - 1)], rs_recv.at[n])
        total = own[col]
        for i in range(1, SIDE):
            total += recv[(col + i) % SIDE].astype(F32)
        out[...] = total.reshape(4, 8, 128)

    for c in range(CHUNKS):
        at = pl.ds(c * tokens, tokens)
        pltpu.make_async_copy(res.at[c], res_hbm.at[at], store_sem.at[0, c]).wait()
        pltpu.make_async_copy(ig.at[c], ig_hbm.at[at], store_sem.at[1, c]).wait()
        for phase, send in enumerate((send_a, send_b, send_c, send_d)):
            wait_bytes(send.at[c, pl.ds(0, 15)], a2a_send.at[phase, c])
    wait_bytes(y_send.at[pl.ds(0, SIDE - 1)], rs_send.at[0])
    wait_bytes(y4_send.at[pl.ds(0, SIDE - 1)], rs_send.at[1])
    wait_bytes(z_send.at[0, pl.ds(0, SIDE - 1)], rs_send.at[2])
    wait_bytes(z_send.at[1, pl.ds(0, SIDE - 1)], rs_send.at[5])
    wait_bytes(z4_send.at[pl.ds(0, SIDE - 1)], rs_send.at[3])
    wait_bytes(y1_send.at[pl.ds(0, SIDE - 1)], rs_send.at[4])
    wait_bytes(z1_send.at[pl.ds(0, SIDE - 1)], rs_send.at[6])


def publish(*refs):
    sources, targets, held, sem = refs[:6], refs[6:12], refs[12:18], refs[18]
    copies = []
    for n, (source, target, slot) in enumerate(zip(sources, targets, held)):
        parts = CHUNKS if n < 2 else 1
        rows = source.shape[0] // parts
        for i in range(parts):
            at = pl.ds(i * rows, rows)
            k = len(copies)
            copies.append((
                pltpu.make_async_copy(source.at[at], slot.at[at], sem.at[0, k]),
                pltpu.make_async_copy(slot.at[at], target.at[at], sem.at[1, k]),
            ))
    for come, _ in copies:
        come.start()
    for come, go in copies:
        come.wait()
        go.start()
    for _, go in copies:
        go.wait()


def local(inputs, cotangent, first_factor, second_factor, third_factor, fourth_factor):
    count, width = inputs.shape
    tokens = count // CHUNKS
    any_spec = pl.BlockSpec(memory_space=pl.ANY)
    vmem = pl.BlockSpec(memory_space=pltpu.VMEM)
    packet = pltpu.VMEM((CHUNKS, 16, 32, tokens), BF)
    block = pltpu.VMEM((CHUNKS, tokens, width), BF)
    outs = (
        jax.ShapeDtypeStruct((count, width), BF),
        jax.ShapeDtypeStruct((count, width), BF),
        jax.ShapeDtypeStruct((4, 8, 128), F32),
        jax.ShapeDtypeStruct((4, 8, 512), F32),
        jax.ShapeDtypeStruct((4, 32, 128), F32),
        jax.ShapeDtypeStruct((4, 8, 128), F32),
    )
    made = pl.pallas_call(
        kernel,
        out_shape=outs,
        in_specs=[any_spec] * 6,
        out_specs=(any_spec, any_spec, vmem, vmem, vmem, vmem),
        scratch_shapes=[
            block, block,
            pltpu.VMEM((4, 128, 128), BF), pltpu.VMEM((4, 128, 512), BF),
            pltpu.VMEM((4, 512, 128), BF), pltpu.VMEM((4, 128, 128), BF),
            pltpu.VMEM((512, 512), BF), pltpu.VMEM((512, 512), BF),
            pltpu.VMEM((2, 256, 1024), BF), pltpu.VMEM((2, 1024, 256), BF),
            pltpu.VMEM((2, 1024, 256), BF), pltpu.VMEM((2, 256, 1024), BF),
            packet, packet, packet, packet, packet, packet, packet, packet,
            pltpu.VMEM((CHUNKS, 2, 1024, tokens), BF), pltpu.VMEM((CHUNKS, 2, 1024, tokens), F32),
            pltpu.VMEM((2, 1024, tokens), BF), block, block,
            pltpu.VMEM((512, 512), F32), pltpu.VMEM((2, 4, 256, 256), F32),
            pltpu.VMEM((2, 1024, 256), F32), pltpu.VMEM((512, 512), F32),
            pltpu.VMEM((SIDE, 2, 128, 512), BF), pltpu.VMEM((SIDE, 2, 128, 512), BF),
            pltpu.VMEM((2, SIDE, 32, 512), BF), pltpu.VMEM((2, SIDE, 32, 512), BF),
            pltpu.VMEM((2, SIDE, 32, 512), F32),
            pltpu.VMEM((SIDE, 128, 128), BF), pltpu.VMEM((SIDE, 128, 128), BF),
            pltpu.VMEM((SIDE, 32, 128), BF), pltpu.VMEM((SIDE, 32, 128), BF),
            pltpu.VMEM((SIDE, 32, 128), F32),
            pltpu.VMEM((SIDE, 128, 128), BF), pltpu.VMEM((SIDE, 128, 128), BF),
            pltpu.VMEM((SIDE, 32, 128), BF), pltpu.VMEM((SIDE, 32, 128), BF),
            pltpu.VMEM((SIDE, 32, 128), F32),
            pltpu.SemaphoreType.DMA((2 * CHUNKS + 4,)), pltpu.SemaphoreType.DMA((2, CHUNKS)),
            pltpu.SemaphoreType.DMA((4, CHUNKS)), pltpu.SemaphoreType.DMA((4, CHUNKS)),
            pltpu.SemaphoreType.DMA((7,)), pltpu.SemaphoreType.DMA((7,)),
        ],
        compiler_params=pltpu.CompilerParams(
            collective_id=0, has_side_effects=True, vmem_limit_bytes=56 * 2**20
        ),
        cost_estimate=pl.CostEstimate(flops=8 * 10**9, bytes_accessed=6 * 10**6, transcendentals=2 * 10**6),
    )(inputs, cotangent, first_factor, second_factor, third_factor, fourth_factor)
    return pl.pallas_call(
        publish,
        out_shape=outs,
        in_specs=[any_spec] * 6,
        out_specs=(any_spec,) * 6,
        scratch_shapes=[pltpu.VMEM(out.shape, out.dtype) for out in outs]
        + [pltpu.SemaphoreType.DMA((2, 2 * CHUNKS + 4))],
        cost_estimate=pl.CostEstimate(flops=0, bytes_accessed=5 * 10**6, transcendentals=0),
    )(*made)


def solution(mesh):
    in_specs = (
        P("dp", "factor"),
        P("dp", "factor"),
        P("factor", None, None),
        P("factor", None, None),
        P("factor", None, None),
        P("factor", None, None),
    )
    out_specs = (
        P("dp", "factor"),
        P("dp", "factor"),
        P("factor", "dp", None),
        P("factor", "dp", None),
        P("factor", "dp", None),
        P("factor", "dp", None),
    )
    return jax.shard_map(local, mesh=mesh, in_specs=in_specs, out_specs=out_specs, check_vma=False)
```

```python
import functools
import math

import jax
import jax.numpy as jnp
from jax import lax
from jax.experimental import pallas as pl
from jax.experimental.pallas import tpu as pltpu
from jax.sharding import PartitionSpec as P

BF = jnp.bfloat16
F32 = jnp.float32
CHUNKS = 1
PIECES = 4
SIDE = 4
HALF = 8
SCALE = math.sqrt(2.0 / math.pi)
CUBE = 0.044715


def nn(a, b):
    return lax.dot_general(a, b, (((1,), (0,)), ((), ())), preferred_element_type=F32)


def nt(a, b):
    return lax.dot_general(a, b, (((1,), (1,)), ((), ())), preferred_element_type=F32)


def tn(a, b):
    return lax.dot_general(a, b, (((0,), (0,)), ((), ())), preferred_element_type=F32)


def iotas(rows, cols, flip):
    axis = 1 if flip else 0
    shape = (cols, rows) if flip else (rows, cols)
    return (
        lax.broadcasted_iota(jnp.int32, shape, axis),
        lax.broadcasted_iota(jnp.int32, shape, 1 - axis),
    )


def one_hot(keep):
    return jnp.where(keep, 1.0, 0.0).astype(BF)


def pick_first(j, flip=False):
    row, k = iotas(512, 128, flip)
    return one_hot(
        (((row >> 2) & 3) == j) & (k == (row >> 5) * 8 + ((row >> 4) & 1) * 4 + (row & 3))
    )


def pick_second(half, flip=False):
    row, m = iotas(256, 128, flip)
    return one_hot((((row >> 1) & 1) == half) & (m == (row & 1) * 64 + (row >> 2)))


def pick_third(half, flip=False):
    row, k = iotas(256, 128, flip)
    return one_hot((((row >> 3) & 1) == half) & (k == (row >> 4) * 8 + (row & 7)))


def pick_fourth(c, flip=False):
    row, m = iotas(512, 128, flip)
    return one_hot(
        (((row >> 1) & 3) == c) & (m == (row & 1) * 64 + (row >> 5) * 4 + ((row >> 3) & 3))
    )


def kernel(
    x_hbm, cot_hbm, w1_hbm, w2_hbm, w3_hbm, w4_hbm,
    res_hbm, ig_hbm, g1_ref, g2_ref, g3_ref, g4_ref,
    x, cot, w1, w2, w3, w4,
    w1r, w4r, w2r, w2t, w3r, w3t,
    send_a, recv_a, send_b, recv_b, send_c, recv_c, send_d, recv_d,
    hidden, slope, grad_pre, res, ig,
    s1, s2, s3, s4,
    y_send, y_recv, z_send, z_recv, z_own,
    y4_send, y4_recv, z4_send, z4_recv, z4_own,
    y1_send, y1_recv, z1_send, z1_recv, z1_own,
    load_sem, store_sem, a2a_send, a2a_recv, rs_send, rs_recv,
):
    tokens = x.shape[1]
    piece = tokens // PIECES
    me = lax.axis_index("factor")
    dp = lax.axis_index("dp")
    half, low = me // HALF, me % HALF
    row, col = dp // SIDE, dp % SIDE

    barrier = pltpu.get_barrier_semaphore()

    loads = []

    def load(src, dst):
        copy = pltpu.make_async_copy(src, dst, load_sem.at[len(loads)])
        copy.start()
        loads.append(copy)
        return copy

    def load_rows(src, dst, c):
        return load(src.at[pl.ds(c * tokens, tokens)], dst.at[c])

    got_w1 = load(w1_hbm, w1)
    got_first = [
        load(x_hbm.at[pl.ds(n * piece, piece)], x.at[0, pl.ds(n * piece, piece)]) for n in range(PIECES)
    ]
    got_x = []

    def greet(i, _):
        pl.semaphore_signal(barrier, inc=1, device_id={"factor": (me + i) % 16}, device_id_type=pl.DeviceIdType.MESH)
        return 0

    def greet_dp(i, _):
        for group in ((row + i) % SIDE * SIDE + col, row * SIDE + (col + i) % SIDE):
            pl.semaphore_signal(barrier, inc=1, device_id={"dp": group}, device_id_type=pl.DeviceIdType.MESH)
        return 0

    lax.fori_loop(1, 16, greet, 0)
    lax.fori_loop(1, SIDE, greet_dp, 0)

    def send_one(phase, c, send, recv, peer):
        pltpu.make_async_remote_copy(
            src_ref=send.at[c, peer], dst_ref=recv.at[c, me],
            send_sem=a2a_send.at[phase, c], recv_sem=a2a_recv.at[phase, c],
            device_id={"factor": peer}, device_id_type=pl.DeviceIdType.MESH,
        ).start()

    def spread_far(phase, c, send, recv):
        def far(i, _):
            send_one(phase, c, send, recv, (1 - half) * HALF + (low + i) % HALF)
            return 0

        lax.fori_loop(0, HALF, far, 0)

    def spread_near(phase, c, send, recv):
        recv[c, me] = send[c, me]

        def near(i, _):
            send_one(phase, c, send, recv, half * HALF + (low + i) % HALF)
            return 0

        lax.fori_loop(1, HALF, near, 0)

    def spread(phase, c, send, recv):
        spread_far(phase, c, send, recv)
        spread_near(phase, c, send, recv)

    def wait_bytes(ref, sem):
        pltpu.make_async_copy(ref, ref, sem).wait()

    def arrived(phase, c, recv):
        wait_bytes(recv.at[c, pl.ds(0, 15)], a2a_recv.at[phase, c])

    got_w1.wait()
    for j in range(4):
        w1r[:, j * 128 : (j + 1) * 128] = nt(pick_first(j), w1[j]).astype(BF)

    def rows_of(side):
        return w1r[pl.ds(pl.multiple_of(side * 256, 256), 256), :]

    for n, got in enumerate(got_first):
        got.wait()
        at = slice(n * piece, (n + 1) * piece)
        send_a[0, pl.ds((1 - half) * HALF, HALF), :, at] = (
            nt(rows_of(1 - half), x[0, at]).astype(BF).reshape(HALF, 32, piece)
        )
    got_x += [load_rows(x_hbm, x, n) for n in range(1, CHUNKS)]
    got_w4 = load(w4_hbm, w4)
    got_cot = [load_rows(cot_hbm, cot, n) for n in range(CHUNKS)]
    got_w2 = load(w2_hbm, w2)
    got_w3 = load(w3_hbm, w3)
    pl.semaphore_wait(barrier, 15 + 2 * (SIDE - 1))
    spread_far(0, 0, send_a, recv_a)
    send_a[0, pl.ds(half * HALF, HALF)] = nt(rows_of(half), x[0]).astype(BF).reshape(HALF, 32, tokens)
    spread_near(0, 0, send_a, recv_a)
    for c in range(1, CHUNKS):
        got_x[c - 1].wait()
        send_a[c] = nt(w1r[...], x[c]).astype(BF).reshape(16, 32, tokens)
        spread(0, c, send_a, recv_a)

    got_w4.wait()
    for c in range(4):
        w4r[:, c * 128 : (c + 1) * 128] = nn(pick_fourth(c), w4[c]).astype(BF)
    for c in range(CHUNKS):
        got_cot[c].wait()
        send_b[c] = nt(w4r[...], cot[c]).astype(BF).reshape(16, 32, tokens)
        spread(1, c, send_b, recv_b)

    got_w2.wait()
    got_w3.wait()
    for p in range(2):
        for h in range(2):
            b = 2 * p + h
            w2r[p, :, h * 512 : (h + 1) * 512] = nn(pick_second(h), w2[b]).astype(BF)
            w2t[p, h * 512 : (h + 1) * 512, :] = tn(w2[b], pick_second(h, True)).astype(BF)
            w3r[p, h * 512 : (h + 1) * 512, :] = nn(w3[b], pick_third(h, True)).astype(BF)
            w3t[p, :, h * 512 : (h + 1) * 512] = nt(pick_third(h), w3[b]).astype(BF)
    s1[...] = jnp.zeros_like(s1)
    s2[...] = jnp.zeros_like(s2)
    s3[...] = jnp.zeros_like(s3)
    s4[...] = jnp.zeros_like(s4)

    def pair_rows(ref, c, p):
        return ref[c, :, pl.ds(p * 16, 16), :].reshape(256, tokens)

    def forward(c, _):
        arrived(0, c, recv_a)
        for p in range(2):
            mixed = pair_rows(recv_a, c, p)

            def tile(o, _):
                at = pl.ds(pl.multiple_of(o * 256, 256), 256)
                v = nn(w2t[p, at, :], mixed)
                sq = v * v
                t = jnp.tanh(v * (SCALE + (SCALE * CUBE) * sq))
                cdf = 0.5 + 0.5 * t
                hidden[c, p, at, :] = (v * cdf).astype(BF)
                slope[c, p, at, :] = cdf + (0.5 * v) * (1.0 - t * t) * (SCALE + (3.0 * SCALE * CUBE) * sq)
                return 0

            lax.fori_loop(0, 4, tile, 0)
            third = nn(w3t[p], hidden[c, p]).astype(BF)
            send_c[c, :, p * 16 : (p + 1) * 16, :] = third.reshape(16, 16, tokens)
        spread(2, c, send_c, recv_c)
        return 0

    lax.fori_loop(0, CHUNKS, forward, 0)

    def backward(c, _):
        arrived(1, c, recv_b)
        for p in range(2):
            back = pair_rows(recv_b, c, p)

            def tile(o, _):
                at = pl.ds(pl.multiple_of(o * 256, 256), 256)
                grad_pre[p, at, :] = (nn(w3r[p, at, :], back) * slope[c, p, at, :]).astype(BF)
                return 0

            lax.fori_loop(0, 4, tile, 0)
            first = nn(w2r[p], grad_pre[p]).astype(BF)
            send_d[c, :, p * 16 : (p + 1) * 16, :] = first.reshape(16, 16, tokens)
        spread(3, c, send_d, recv_d)
        for p in range(2):
            back = pair_rows(recv_b, c, p)
            mixed = pair_rows(recv_a, c, p)

            def sums(o, _):
                at = pl.ds(pl.multiple_of(o * 256, 256), 256)
                s3[p, at, :] += nt(hidden[c, p, at, :], back)
                s2[p, o] += nt(mixed, grad_pre[p, at, :])
                return 0

            lax.fori_loop(0, 4, sums, 0)
        return 0

    lax.fori_loop(0, CHUNKS, backward, 0)

    def scatter(n, at, members, stride, base, send, recv):
        def one(i, _):
            peer = (at + i) % members
            pltpu.make_async_remote_copy(
                src_ref=send.at[peer], dst_ref=recv.at[at],
                send_sem=rs_send.at[n], recv_sem=rs_recv.at[n],
                device_id={"dp": base + peer * stride}, device_id_type=pl.DeviceIdType.MESH,
            ).start()
            return 0

        lax.fori_loop(1, members, one, 0)

    def scatter_y(n, send, recv):
        scatter(n, row, SIDE, SIDE, col, send, recv)

    def scatter_z(n, send, recv):
        scatter(n, col, SIDE, 1, row * SIDE, send, recv)

    for b in range(4):
        p, h = b // 2, b % 2
        third = s3[p, h * 512 : (h + 1) * 512, :].astype(BF)
        y_send[:, 1, :, b * 128 : (b + 1) * 128] = (
            nn(third, pick_third(h)).astype(BF).reshape(4, 128, 128)
        )
    for o in range(2):
        parts = [
            nn(pick_second(b % 2, True), s2[b // 2, 2 * (b % 2) + o].astype(BF)).reshape(16, 1, 8, 256)
            for b in range(4)
        ]
        y_send[:, 0, :, o * 256 : (o + 1) * 256] = (
            jnp.concatenate(parts, axis=1).reshape(4, 128, 256).astype(BF)
        )
    scatter_y(0, y_send, y_recv)

    def last_forward(c, _):
        arrived(2, c, recv_c)
        mixed = recv_c[c].reshape(512, tokens)
        res[c] = tn(mixed, w4r[...]).astype(BF)
        at = pl.ds(pl.multiple_of(c * tokens, tokens), tokens)
        pltpu.make_async_copy(res.at[c], res_hbm.at[at], store_sem.at[0, c]).start()
        s4[...] += nn(mixed, cot[c])
        return 0

    lax.fori_loop(0, CHUNKS, last_forward, 0)

    def own_rows(parts):
        return jnp.concatenate([v.reshape(16, 1, 8, 128) for v in parts], axis=1)

    parts = [nn(pick_fourth(c, True), s4[:, c * 128 : (c + 1) * 128].astype(BF)) for c in range(4)]
    y4_send[...] = own_rows(parts).reshape(4, 128, 128).astype(BF)
    scatter_y(1, y4_send, y4_recv)

    wait_bytes(y_recv.at[pl.ds(0, SIDE - 1)], rs_recv.at[0])
    for n in range(2):
        total = y_send[row, n].astype(F32)
        for i in range(1, SIDE):
            total += y_recv[(row + i) % SIDE, n].astype(F32)
        z_send[n] = total.astype(BF).reshape(SIDE, 32, 512)
        z_own[n] = total.reshape(SIDE, 32, 512)

    def stored(c, n):
        at = pl.ds(c * tokens + n * piece, piece)
        return pltpu.make_async_copy(ig.at[c, pl.ds(n * piece, piece)], ig_hbm.at[at], store_sem.at[1, c * PIECES + n])

    def input_rows(c, pieces):
        for n in pieces:
            at = slice(n * piece, (n + 1) * piece)
            ig[c, at] = tn(recv_d[c, :, :, at].reshape(512, piece), w1r[...]).astype(BF)
            stored(c, n).start()

    def last_backward(c, _):
        arrived(3, c, recv_d)
        s1[...] += nn(recv_d[c].reshape(512, tokens), x[c])
        input_rows(c, range(PIECES))
        return 0

    lax.fori_loop(0, CHUNKS - 1, last_backward, 0)

    def fold(n, y_out, y_in, z_out, own):
        wait_bytes(y_in.at[pl.ds(0, SIDE - 1)], rs_recv.at[n])
        total = y_out[row].astype(F32)
        for i in range(1, SIDE):
            total += y_in[(row + i) % SIDE].astype(F32)
        z_out[...] = total.astype(BF).reshape(SIDE, 32, 128)
        own[...] = total.reshape(SIDE, 32, 128)

    fold(1, y4_send, y4_recv, z4_send, z4_own)

    arrived(3, CHUNKS - 1, recv_d)
    scatter_z(2, z_send.at[0], z_recv.at[0])
    scatter_z(5, z_send.at[1], z_recv.at[1])
    scatter_z(3, z4_send, z4_recv)
    s1[...] += nn(recv_d[CHUNKS - 1].reshape(512, tokens), x[CHUNKS - 1])
    parts = [tn(s1[:, j * 128 : (j + 1) * 128].astype(BF), pick_first(j)) for j in range(4)]
    y1_send[...] = own_rows(parts).reshape(4, 128, 128).astype(BF)
    scatter_y(4, y1_send, y1_recv)
    input_rows(CHUNKS - 1, range(PIECES // 2))
    fold(4, y1_send, y1_recv, z1_send, z1_own)
    scatter_z(6, z1_send, z1_recv)
    input_rows(CHUNKS - 1, range(PIECES // 2, PIECES))

    for n in range(2):
        wait_bytes(z_recv.at[n, pl.ds(0, SIDE - 1)], rs_recv.at[(2, 5)[n]])
        total = z_own[n, col]
        for i in range(1, SIDE):
            total += z_recv[n, (col + i) % SIDE].astype(F32)
        if n == 0:
            g2_ref[...] = total.reshape(4, 8, 512)
        else:
            for j in range(4):
                g3_ref[j] = total[:, j * 128 : (j + 1) * 128]

    for n, own, recv, out in ((3, z4_own, z4_recv, g4_ref), (6, z1_own, z1_recv, g1_ref)):
        wait_bytes(recv.at[pl.ds(0, SIDE - 1)], rs_recv.at[n])
        total = own[col]
        for i in range(1, SIDE):
            total += recv[(col + i) % SIDE].astype(F32)
        out[...] = total.reshape(4, 8, 128)

    for c in range(CHUNKS):
        at = pl.ds(c * tokens, tokens)
        pltpu.make_async_copy(res.at[c], res_hbm.at[at], store_sem.at[0, c]).wait()
        for n in range(PIECES):
            stored(c, n).wait()
        for phase, send in enumerate((send_a, send_b, send_c, send_d)):
            wait_bytes(send.at[c, pl.ds(0, 15)], a2a_send.at[phase, c])
    wait_bytes(y_send.at[pl.ds(0, SIDE - 1)], rs_send.at[0])
    wait_bytes(y4_send.at[pl.ds(0, SIDE - 1)], rs_send.at[1])
    wait_bytes(z_send.at[0, pl.ds(0, SIDE - 1)], rs_send.at[2])
    wait_bytes(z_send.at[1, pl.ds(0, SIDE - 1)], rs_send.at[5])
    wait_bytes(z4_send.at[pl.ds(0, SIDE - 1)], rs_send.at[3])
    wait_bytes(y1_send.at[pl.ds(0, SIDE - 1)], rs_send.at[4])
    wait_bytes(z1_send.at[pl.ds(0, SIDE - 1)], rs_send.at[6])


def publish(*refs):
    sources, targets, held, sem = refs[:6], refs[6:12], refs[12:18], refs[18]
    copies = []
    for n, (source, target, slot) in enumerate(zip(sources, targets, held)):
        parts = CHUNKS if n < 2 else 1
        rows = source.shape[0] // parts
        for i in range(parts):
            at = pl.ds(i * rows, rows)
            k = len(copies)
            copies.append((
                pltpu.make_async_copy(source.at[at], slot.at[at], sem.at[0, k]),
                pltpu.make_async_copy(slot.at[at], target.at[at], sem.at[1, k]),
            ))
    for come, _ in copies:
        come.start()
    for come, go in copies:
        come.wait()
        go.start()
    for _, go in copies:
        go.wait()


def local(inputs, cotangent, first_factor, second_factor, third_factor, fourth_factor):
    count, width = inputs.shape
    tokens = count // CHUNKS
    any_spec = pl.BlockSpec(memory_space=pl.ANY)
    vmem = pl.BlockSpec(memory_space=pltpu.VMEM)
    packet = pltpu.VMEM((CHUNKS, 16, 32, tokens), BF)
    block = pltpu.VMEM((CHUNKS, tokens, width), BF)
    outs = (
        jax.ShapeDtypeStruct((count, width), BF),
        jax.ShapeDtypeStruct((count, width), BF),
        jax.ShapeDtypeStruct((4, 8, 128), F32),
        jax.ShapeDtypeStruct((4, 8, 512), F32),
        jax.ShapeDtypeStruct((4, 32, 128), F32),
        jax.ShapeDtypeStruct((4, 8, 128), F32),
    )
    made = pl.pallas_call(
        kernel,
        out_shape=outs,
        in_specs=[any_spec] * 6,
        out_specs=(any_spec, any_spec, vmem, vmem, vmem, vmem),
        scratch_shapes=[
            block, block,
            pltpu.VMEM((4, 128, 128), BF), pltpu.VMEM((4, 128, 512), BF),
            pltpu.VMEM((4, 512, 128), BF), pltpu.VMEM((4, 128, 128), BF),
            pltpu.VMEM((512, 512), BF), pltpu.VMEM((512, 512), BF),
            pltpu.VMEM((2, 256, 1024), BF), pltpu.VMEM((2, 1024, 256), BF),
            pltpu.VMEM((2, 1024, 256), BF), pltpu.VMEM((2, 256, 1024), BF),
            packet, packet, packet, packet, packet, packet, packet, packet,
            pltpu.VMEM((CHUNKS, 2, 1024, tokens), BF), pltpu.VMEM((CHUNKS, 2, 1024, tokens), F32),
            pltpu.VMEM((2, 1024, tokens), BF), block, block,
            pltpu.VMEM((512, 512), F32), pltpu.VMEM((2, 4, 256, 256), F32),
            pltpu.VMEM((2, 1024, 256), F32), pltpu.VMEM((512, 512), F32),
            pltpu.VMEM((SIDE, 2, 128, 512), BF), pltpu.VMEM((SIDE, 2, 128, 512), BF),
            pltpu.VMEM((2, SIDE, 32, 512), BF), pltpu.VMEM((2, SIDE, 32, 512), BF),
            pltpu.VMEM((2, SIDE, 32, 512), F32),
            pltpu.VMEM((SIDE, 128, 128), BF), pltpu.VMEM((SIDE, 128, 128), BF),
            pltpu.VMEM((SIDE, 32, 128), BF), pltpu.VMEM((SIDE, 32, 128), BF),
            pltpu.VMEM((SIDE, 32, 128), F32),
            pltpu.VMEM((SIDE, 128, 128), BF), pltpu.VMEM((SIDE, 128, 128), BF),
            pltpu.VMEM((SIDE, 32, 128), BF), pltpu.VMEM((SIDE, 32, 128), BF),
            pltpu.VMEM((SIDE, 32, 128), F32),
            pltpu.SemaphoreType.DMA((2 * CHUNKS + 3 + PIECES,)), pltpu.SemaphoreType.DMA((2, CHUNKS * PIECES)),
            pltpu.SemaphoreType.DMA((4, CHUNKS)), pltpu.SemaphoreType.DMA((4, CHUNKS)),
            pltpu.SemaphoreType.DMA((7,)), pltpu.SemaphoreType.DMA((7,)),
        ],
        compiler_params=pltpu.CompilerParams(
            collective_id=0, has_side_effects=True, vmem_limit_bytes=56 * 2**20
        ),
        cost_estimate=pl.CostEstimate(flops=8 * 10**9, bytes_accessed=6 * 10**6, transcendentals=2 * 10**6),
    )(inputs, cotangent, first_factor, second_factor, third_factor, fourth_factor)
    return pl.pallas_call(
        publish,
        out_shape=outs,
        in_specs=[any_spec] * 6,
        out_specs=(any_spec,) * 6,
        scratch_shapes=[pltpu.VMEM(out.shape, out.dtype) for out in outs]
        + [pltpu.SemaphoreType.DMA((2, 2 * CHUNKS + 4))],
        cost_estimate=pl.CostEstimate(flops=0, bytes_accessed=5 * 10**6, transcendentals=0),
    )(*made)


def solution(mesh):
    in_specs = (
        P("dp", "factor"),
        P("dp", "factor"),
        P("factor", None, None),
        P("factor", None, None),
        P("factor", None, None),
        P("factor", None, None),
    )
    out_specs = (
        P("dp", "factor"),
        P("dp", "factor"),
        P("factor", "dp", None),
        P("factor", "dp", None),
        P("factor", "dp", None),
        P("factor", "dp", None),
    )
    return jax.shard_map(local, mesh=mesh, in_specs=in_specs, out_specs=out_specs, check_vma=False)
```

```python
import functools
import math

import jax
import jax.numpy as jnp
from jax import lax
from jax.experimental import pallas as pl
from jax.experimental.pallas import tpu as pltpu
from jax.sharding import PartitionSpec as P

BF = jnp.bfloat16
F32 = jnp.float32
CHUNKS = 1
PIECES = 4
SIDE = 4
HALF = 8
SCALE = math.sqrt(2.0 / math.pi)
CUBE = 0.044715


def nn(a, b):
    return lax.dot_general(a, b, (((1,), (0,)), ((), ())), preferred_element_type=F32)


def nt(a, b):
    return lax.dot_general(a, b, (((1,), (1,)), ((), ())), preferred_element_type=F32)


def tn(a, b):
    return lax.dot_general(a, b, (((0,), (0,)), ((), ())), preferred_element_type=F32)


def iotas(rows, cols, flip):
    axis = 1 if flip else 0
    shape = (cols, rows) if flip else (rows, cols)
    return (
        lax.broadcasted_iota(jnp.int32, shape, axis),
        lax.broadcasted_iota(jnp.int32, shape, 1 - axis),
    )


def one_hot(keep):
    return jnp.where(keep, 1.0, 0.0).astype(BF)


def pick_first(j, flip=False):
    row, k = iotas(512, 128, flip)
    return one_hot(
        (((row >> 2) & 3) == j) & (k == (row >> 5) * 8 + ((row >> 4) & 1) * 4 + (row & 3))
    )


def pick_second(half, flip=False):
    row, m = iotas(256, 128, flip)
    return one_hot((((row >> 1) & 1) == half) & (m == (row & 1) * 64 + (row >> 2)))


def pick_third(half, flip=False):
    row, k = iotas(256, 128, flip)
    return one_hot((((row >> 3) & 1) == half) & (k == (row >> 4) * 8 + (row & 7)))


def pick_fourth(c, flip=False):
    row, m = iotas(512, 128, flip)
    return one_hot(
        (((row >> 1) & 3) == c) & (m == (row & 1) * 64 + (row >> 5) * 4 + ((row >> 3) & 3))
    )


def kernel(
    x_hbm, cot_hbm, w1_hbm, w2_hbm, w3_hbm, w4_hbm,
    res_hbm, ig_hbm, g1_ref, g2_ref, g3_ref, g4_ref,
    x, cot, w1, w2, w3, w4,
    w1r, w4r, w2r, w2t, w3r, w3t,
    send_a, recv_a, send_b, recv_b, send_c, recv_c, send_d, recv_d,
    hidden, slope, grad_pre, res, ig,
    s1, s2, s3, s4,
    y_send, y_recv, z_send, z_recv, z_own,
    y4_send, y4_recv, z4_send, z4_recv, z4_own,
    y1_send, y1_recv, z1_send, z1_recv, z1_own,
    load_sem, store_sem, a2a_send, a2a_recv, rs_send, rs_recv,
):
    tokens = x.shape[1]
    piece = tokens // PIECES
    me = lax.axis_index("factor")
    dp = lax.axis_index("dp")
    half, low = me // HALF, me % HALF
    row, col = dp // SIDE, dp % SIDE

    barrier = pltpu.get_barrier_semaphore()

    loads = []

    def load(src, dst):
        copy = pltpu.make_async_copy(src, dst, load_sem.at[len(loads)])
        copy.start()
        loads.append(copy)
        return copy

    def load_rows(src, dst, c):
        return load(src.at[pl.ds(c * tokens, tokens)], dst.at[c])

    got_w1 = load(w1_hbm, w1)
    got_first = [
        load(x_hbm.at[pl.ds(n * piece, piece)], x.at[0, pl.ds(n * piece, piece)]) for n in range(PIECES)
    ]
    got_x = []

    def greet(i, _):
        pl.semaphore_signal(barrier, inc=1, device_id={"factor": (me + i) % 16}, device_id_type=pl.DeviceIdType.MESH)
        return 0

    def greet_dp(i, _):
        for group in ((row + i) % SIDE * SIDE + col, row * SIDE + (col + i) % SIDE):
            pl.semaphore_signal(barrier, inc=1, device_id={"dp": group}, device_id_type=pl.DeviceIdType.MESH)
        return 0

    lax.fori_loop(1, 16, greet, 0)
    lax.fori_loop(1, SIDE, greet_dp, 0)

    def send_one(phase, c, send, recv, peer):
        pltpu.make_async_remote_copy(
            src_ref=send.at[c, peer], dst_ref=recv.at[c, me],
            send_sem=a2a_send.at[phase, c], recv_sem=a2a_recv.at[phase, c],
            device_id={"factor": peer}, device_id_type=pl.DeviceIdType.MESH,
        ).start()

    def spread_far(phase, c, send, recv):
        def far(i, _):
            send_one(phase, c, send, recv, (1 - half) * HALF + (low + i) % HALF)
            return 0

        lax.fori_loop(0, HALF, far, 0)

    def spread_near(phase, c, send, recv):
        recv[c, me] = send[c, me]

        def near(i, _):
            send_one(phase, c, send, recv, half * HALF + (low + i) % HALF)
            return 0

        lax.fori_loop(1, HALF, near, 0)

    def spread(phase, c, send, recv):
        spread_far(phase, c, send, recv)
        spread_near(phase, c, send, recv)

    def wait_bytes(ref, sem):
        pltpu.make_async_copy(ref, ref, sem).wait()

    def arrived(phase, c, recv):
        wait_bytes(recv.at[c, pl.ds(0, 15)], a2a_recv.at[phase, c])

    got_w1.wait()
    for j in range(4):
        w1r[:, j * 128 : (j + 1) * 128] = nt(pick_first(j), w1[j]).astype(BF)

    def rows_of(side):
        return w1r[pl.ds(pl.multiple_of(side * 256, 256), 256), :]

    for n, got in enumerate(got_first):
        got.wait()
        at = slice(n * piece, (n + 1) * piece)
        send_a[0, pl.ds((1 - half) * HALF, HALF), :, at] = (
            nt(rows_of(1 - half), x[0, at]).astype(BF).reshape(HALF, 32, piece)
        )
    got_x += [load_rows(x_hbm, x, n) for n in range(1, CHUNKS)]
    got_w4 = load(w4_hbm, w4)
    got_cot = [load_rows(cot_hbm, cot, n) for n in range(CHUNKS)]
    got_w2 = load(w2_hbm, w2)
    got_w3 = load(w3_hbm, w3)
    pl.semaphore_wait(barrier, 15 + 2 * (SIDE - 1))
    spread_far(0, 0, send_a, recv_a)
    send_a[0, pl.ds(half * HALF, HALF)] = nt(rows_of(half), x[0]).astype(BF).reshape(HALF, 32, tokens)
    spread_near(0, 0, send_a, recv_a)
    for c in range(1, CHUNKS):
        got_x[c - 1].wait()
        send_a[c] = nt(w1r[...], x[c]).astype(BF).reshape(16, 32, tokens)
        spread(0, c, send_a, recv_a)

    got_w4.wait()
    for c in range(4):
        w4r[:, c * 128 : (c + 1) * 128] = nn(pick_fourth(c), w4[c]).astype(BF)
    for c in range(CHUNKS):
        got_cot[c].wait()
        send_b[c] = nt(w4r[...], cot[c]).astype(BF).reshape(16, 32, tokens)
        spread(1, c, send_b, recv_b)

    got_w2.wait()
    got_w3.wait()
    for p in range(2):
        for h in range(2):
            b = 2 * p + h
            w2r[p, :, h * 512 : (h + 1) * 512] = nn(pick_second(h), w2[b]).astype(BF)
            w2t[p, h * 512 : (h + 1) * 512, :] = tn(w2[b], pick_second(h, True)).astype(BF)
            w3r[p, h * 512 : (h + 1) * 512, :] = nn(w3[b], pick_third(h, True)).astype(BF)
            w3t[p, :, h * 512 : (h + 1) * 512] = nt(pick_third(h), w3[b]).astype(BF)
    s1[...] = jnp.zeros_like(s1)
    s2[...] = jnp.zeros_like(s2)
    s3[...] = jnp.zeros_like(s3)
    s4[...] = jnp.zeros_like(s4)

    def pair_rows(ref, c, p):
        return ref[c, :, pl.ds(p * 16, 16), :].reshape(256, tokens)

    def forward(c, _):
        arrived(0, c, recv_a)
        for p in range(2):
            mixed = pair_rows(recv_a, c, p)

            def tile(o, _):
                at = pl.ds(pl.multiple_of(o * 256, 256), 256)
                v = nn(w2t[p, at, :], mixed)
                sq = v * v
                t = jnp.tanh(v * (SCALE + (SCALE * CUBE) * sq))
                cdf = 0.5 + 0.5 * t
                hidden[c, p, at, :] = (v * cdf).astype(BF)
                slope[c, p, at, :] = cdf + (0.5 * v) * (1.0 - t * t) * (SCALE + (3.0 * SCALE * CUBE) * sq)
                return 0

            lax.fori_loop(0, 4, tile, 0)
            third = nn(w3t[p], hidden[c, p]).astype(BF)
            send_c[c, :, p * 16 : (p + 1) * 16, :] = third.reshape(16, 16, tokens)
        spread(2, c, send_c, recv_c)
        return 0

    lax.fori_loop(0, CHUNKS, forward, 0)

    def backward(c, _):
        arrived(1, c, recv_b)
        for p in range(2):
            back = pair_rows(recv_b, c, p)

            def tile(o, _):
                at = pl.ds(pl.multiple_of(o * 256, 256), 256)
                grad_pre[p, at, :] = (nn(w3r[p, at, :], back) * slope[c, p, at, :]).astype(BF)
                return 0

            lax.fori_loop(0, 4, tile, 0)
            first = nn(w2r[p], grad_pre[p]).astype(BF)
            send_d[c, :, p * 16 : (p + 1) * 16, :] = first.reshape(16, 16, tokens)
        spread(3, c, send_d, recv_d)
        for p in range(2):
            back = pair_rows(recv_b, c, p)
            mixed = pair_rows(recv_a, c, p)

            def sums(o, _):
                at = pl.ds(pl.multiple_of(o * 256, 256), 256)
                s3[p, at, :] += nt(hidden[c, p, at, :], back)
                s2[p, o] += nt(mixed, grad_pre[p, at, :])
                return 0

            lax.fori_loop(0, 4, sums, 0)
        return 0

    lax.fori_loop(0, CHUNKS, backward, 0)

    def scatter(n, at, members, stride, base, send, recv):
        def one(i, _):
            peer = (at + i) % members
            pltpu.make_async_remote_copy(
                src_ref=send.at[peer], dst_ref=recv.at[at],
                send_sem=rs_send.at[n], recv_sem=rs_recv.at[n],
                device_id={"dp": base + peer * stride}, device_id_type=pl.DeviceIdType.MESH,
            ).start()
            return 0

        lax.fori_loop(1, members, one, 0)

    def scatter_y(n, send, recv):
        scatter(n, row, SIDE, SIDE, col, send, recv)

    def scatter_z(n, send, recv):
        scatter(n, col, SIDE, 1, row * SIDE, send, recv)

    for b in range(4):
        p, h = b // 2, b % 2
        third = s3[p, h * 512 : (h + 1) * 512, :].astype(BF)
        y_send[:, 1, :, b * 128 : (b + 1) * 128] = (
            nn(third, pick_third(h)).astype(BF).reshape(4, 128, 128)
        )
    for o in range(2):
        parts = [
            nn(pick_second(b % 2, True), s2[b // 2, 2 * (b % 2) + o].astype(BF)).reshape(16, 1, 8, 256)
            for b in range(4)
        ]
        y_send[:, 0, :, o * 256 : (o + 1) * 256] = (
            jnp.concatenate(parts, axis=1).reshape(4, 128, 256).astype(BF)
        )
    scatter_y(0, y_send, y_recv)

    def last_forward(c, _):
        arrived(2, c, recv_c)
        mixed = recv_c[c].reshape(512, tokens)
        res[c] = tn(mixed, w4r[...]).astype(BF)
        at = pl.ds(pl.multiple_of(c * tokens, tokens), tokens)
        pltpu.make_async_copy(res.at[c], res_hbm.at[at], store_sem.at[0, c]).start()
        s4[...] += nn(mixed, cot[c])
        return 0

    lax.fori_loop(0, CHUNKS, last_forward, 0)

    def own_rows(parts):
        return jnp.concatenate([v.reshape(16, 1, 8, 128) for v in parts], axis=1)

    parts = [nn(pick_fourth(c, True), s4[:, c * 128 : (c + 1) * 128].astype(BF)) for c in range(4)]
    y4_send[...] = own_rows(parts).reshape(4, 128, 128).astype(BF)
    scatter_y(1, y4_send, y4_recv)

    wait_bytes(y_recv.at[pl.ds(0, SIDE - 1)], rs_recv.at[0])
    for n in range(2):
        total = y_send[row, n].astype(F32)
        for i in range(1, SIDE):
            total += y_recv[(row + i) % SIDE, n].astype(F32)
        z_send[n] = total.astype(BF).reshape(SIDE, 32, 512)
        z_own[n] = total.reshape(SIDE, 32, 512)

    def stored(c, n):
        at = pl.ds(c * tokens + n * piece, piece)
        return pltpu.make_async_copy(ig.at[c, pl.ds(n * piece, piece)], ig_hbm.at[at], store_sem.at[1, c * PIECES + n])

    def input_rows(c, pieces):
        for n in pieces:
            at = slice(n * piece, (n + 1) * piece)
            ig[c, at] = tn(recv_d[c, :, :, at].reshape(512, piece), w1r[...]).astype(BF)
            stored(c, n).start()

    def last_backward(c, _):
        arrived(3, c, recv_d)
        s1[...] += nn(recv_d[c].reshape(512, tokens), x[c])
        input_rows(c, range(PIECES))
        return 0

    lax.fori_loop(0, CHUNKS - 1, last_backward, 0)

    def fold(n, y_out, y_in, z_out, own):
        wait_bytes(y_in.at[pl.ds(0, SIDE - 1)], rs_recv.at[n])
        total = y_out[row].astype(F32)
        for i in range(1, SIDE):
            total += y_in[(row + i) % SIDE].astype(F32)
        z_out[...] = total.astype(BF).reshape(SIDE, 32, 128)
        own[...] = total.reshape(SIDE, 32, 128)

    fold(1, y4_send, y4_recv, z4_send, z4_own)

    arrived(3, CHUNKS - 1, recv_d)
    scatter_z(2, z_send.at[0], z_recv.at[0])
    scatter_z(5, z_send.at[1], z_recv.at[1])
    scatter_z(3, z4_send, z4_recv)
    s1[...] += nn(recv_d[CHUNKS - 1].reshape(512, tokens), x[CHUNKS - 1])
    parts = [tn(s1[:, j * 128 : (j + 1) * 128].astype(BF), pick_first(j)) for j in range(4)]
    y1_send[...] = own_rows(parts).reshape(4, 128, 128).astype(BF)
    scatter_y(4, y1_send, y1_recv)
    input_rows(CHUNKS - 1, range(PIECES // 2))
    fold(4, y1_send, y1_recv, z1_send, z1_own)
    scatter_z(6, z1_send, z1_recv)
    input_rows(CHUNKS - 1, range(PIECES // 2, PIECES))

    for n in range(2):
        wait_bytes(z_recv.at[n, pl.ds(0, SIDE - 1)], rs_recv.at[(2, 5)[n]])
        total = z_own[n, col]
        for i in range(1, SIDE):
            total += z_recv[n, (col + i) % SIDE].astype(F32)
        if n == 0:
            g2_ref[...] = total.reshape(4, 8, 512)
        else:
            for j in range(4):
                g3_ref[j] = total[:, j * 128 : (j + 1) * 128]

    for n, own, recv, out in ((3, z4_own, z4_recv, g4_ref), (6, z1_own, z1_recv, g1_ref)):
        wait_bytes(recv.at[pl.ds(0, SIDE - 1)], rs_recv.at[n])
        total = own[col]
        for i in range(1, SIDE):
            total += recv[(col + i) % SIDE].astype(F32)
        out[...] = total.reshape(4, 8, 128)

    for c in range(CHUNKS):
        at = pl.ds(c * tokens, tokens)
        pltpu.make_async_copy(res.at[c], res_hbm.at[at], store_sem.at[0, c]).wait()
        for n in range(PIECES):
            stored(c, n).wait()
        for phase, send in enumerate((send_a, send_b, send_c, send_d)):
            wait_bytes(send.at[c, pl.ds(0, 15)], a2a_send.at[phase, c])
    wait_bytes(y_send.at[pl.ds(0, SIDE - 1)], rs_send.at[0])
    wait_bytes(y4_send.at[pl.ds(0, SIDE - 1)], rs_send.at[1])
    wait_bytes(z_send.at[0, pl.ds(0, SIDE - 1)], rs_send.at[2])
    wait_bytes(z_send.at[1, pl.ds(0, SIDE - 1)], rs_send.at[5])
    wait_bytes(z4_send.at[pl.ds(0, SIDE - 1)], rs_send.at[3])
    wait_bytes(y1_send.at[pl.ds(0, SIDE - 1)], rs_send.at[4])
    wait_bytes(z1_send.at[pl.ds(0, SIDE - 1)], rs_send.at[6])


def publish(*refs):
    sources, targets, held, sem = refs[:6], refs[6:12], refs[12:18], refs[18]
    copies = []
    for n, (source, target, slot) in enumerate(zip(sources, targets, held)):
        parts = PIECES if n < 2 else 1
        rows = source.shape[0] // parts
        for i in range(parts):
            at = pl.ds(i * rows, rows)
            k = len(copies)
            copies.append((
                pltpu.make_async_copy(source.at[at], slot.at[at], sem.at[0, k]),
                pltpu.make_async_copy(slot.at[at], target.at[at], sem.at[1, k]),
            ))
    for come, _ in copies:
        come.start()
    for come, go in copies:
        come.wait()
        go.start()
    for _, go in copies:
        go.wait()


def local(inputs, cotangent, first_factor, second_factor, third_factor, fourth_factor):
    count, width = inputs.shape
    tokens = count // CHUNKS
    any_spec = pl.BlockSpec(memory_space=pl.ANY)
    vmem = pl.BlockSpec(memory_space=pltpu.VMEM)
    packet = pltpu.VMEM((CHUNKS, 16, 32, tokens), BF)
    block = pltpu.VMEM((CHUNKS, tokens, width), BF)
    outs = (
        jax.ShapeDtypeStruct((count, width), BF),
        jax.ShapeDtypeStruct((count, width), BF),
        jax.ShapeDtypeStruct((4, 8, 128), F32),
        jax.ShapeDtypeStruct((4, 8, 512), F32),
        jax.ShapeDtypeStruct((4, 32, 128), F32),
        jax.ShapeDtypeStruct((4, 8, 128), F32),
    )
    made = pl.pallas_call(
        kernel,
        out_shape=outs,
        in_specs=[any_spec] * 6,
        out_specs=(any_spec, any_spec, vmem, vmem, vmem, vmem),
        scratch_shapes=[
            block, block,
            pltpu.VMEM((4, 128, 128), BF), pltpu.VMEM((4, 128, 512), BF),
            pltpu.VMEM((4, 512, 128), BF), pltpu.VMEM((4, 128, 128), BF),
            pltpu.VMEM((512, 512), BF), pltpu.VMEM((512, 512), BF),
            pltpu.VMEM((2, 256, 1024), BF), pltpu.VMEM((2, 1024, 256), BF),
            pltpu.VMEM((2, 1024, 256), BF), pltpu.VMEM((2, 256, 1024), BF),
            packet, packet, packet, packet, packet, packet, packet, packet,
            pltpu.VMEM((CHUNKS, 2, 1024, tokens), BF), pltpu.VMEM((CHUNKS, 2, 1024, tokens), F32),
            pltpu.VMEM((2, 1024, tokens), BF), block, block,
            pltpu.VMEM((512, 512), F32), pltpu.VMEM((2, 4, 256, 256), F32),
            pltpu.VMEM((2, 1024, 256), F32), pltpu.VMEM((512, 512), F32),
            pltpu.VMEM((SIDE, 2, 128, 512), BF), pltpu.VMEM((SIDE, 2, 128, 512), BF),
            pltpu.VMEM((2, SIDE, 32, 512), BF), pltpu.VMEM((2, SIDE, 32, 512), BF),
            pltpu.VMEM((2, SIDE, 32, 512), F32),
            pltpu.VMEM((SIDE, 128, 128), BF), pltpu.VMEM((SIDE, 128, 128), BF),
            pltpu.VMEM((SIDE, 32, 128), BF), pltpu.VMEM((SIDE, 32, 128), BF),
            pltpu.VMEM((SIDE, 32, 128), F32),
            pltpu.VMEM((SIDE, 128, 128), BF), pltpu.VMEM((SIDE, 128, 128), BF),
            pltpu.VMEM((SIDE, 32, 128), BF), pltpu.VMEM((SIDE, 32, 128), BF),
            pltpu.VMEM((SIDE, 32, 128), F32),
            pltpu.SemaphoreType.DMA((2 * CHUNKS + 3 + PIECES,)), pltpu.SemaphoreType.DMA((2, CHUNKS * PIECES)),
            pltpu.SemaphoreType.DMA((4, CHUNKS)), pltpu.SemaphoreType.DMA((4, CHUNKS)),
            pltpu.SemaphoreType.DMA((7,)), pltpu.SemaphoreType.DMA((7,)),
        ],
        compiler_params=pltpu.CompilerParams(
            collective_id=0, has_side_effects=True, vmem_limit_bytes=56 * 2**20
        ),
        cost_estimate=pl.CostEstimate(flops=8 * 10**9, bytes_accessed=6 * 10**6, transcendentals=2 * 10**6),
    )(inputs, cotangent, first_factor, second_factor, third_factor, fourth_factor)
    return pl.pallas_call(
        publish,
        out_shape=outs,
        in_specs=[any_spec] * 6,
        out_specs=(any_spec,) * 6,
        scratch_shapes=[pltpu.VMEM(out.shape, out.dtype) for out in outs]
        + [pltpu.SemaphoreType.DMA((2, 2 * PIECES + 4))],
        cost_estimate=pl.CostEstimate(flops=0, bytes_accessed=5 * 10**6, transcendentals=0),
    )(*made)


def solution(mesh):
    in_specs = (
        P("dp", "factor"),
        P("dp", "factor"),
        P("factor", None, None),
        P("factor", None, None),
        P("factor", None, None),
        P("factor", None, None),
    )
    out_specs = (
        P("dp", "factor"),
        P("dp", "factor"),
        P("factor", "dp", None),
        P("factor", "dp", None),
        P("factor", "dp", None),
        P("factor", "dp", None),
    )
    return jax.shard_map(local, mesh=mesh, in_specs=in_specs, out_specs=out_specs, check_vma=False)
```
